128 devices in a mesh: ctx: 16 (over z_hi, y, core), tp: 8 (over z_lo, x).
Axes of the slice: x: 4, y: 4, z: 4 (z_hi: 2, z_lo: 2; z = z_hi * 2 + z_lo), core: 2. Of those that a mesh axis runs over, the one named last changes fastest.
Arguments:
- queries: bfloat16 [1024, 8192], P('ctx', 'tp'), may hold values from -8 to 8
- cache_keys: bfloat16 [65536, 1024], P('ctx', 'tp'), may hold values from -8 to 8
- stored_values: bfloat16 [65536, 1024], P('ctx', 'tp'), may hold values from -6 to 6
- fresh_keys: bfloat16 [1024, 1024], P('ctx', 'tp'), may hold values from -12 to 12
- fresh_values: bfloat16 [1024, 1024], P('ctx', 'tp'), may hold values from -6 to 6
- positions: int32 [1024], P('ctx'), may hold values from 65536 to 66559, as said below
- lengths: int32 [16], P('ctx'), may hold values from 1024 to 4096, as said below
- out_weight: bfloat16 [8192, 8192], P('tp'), may hold values from -0.0625 to 0.0625
Outputs:
- attended_out: bfloat16 [1024, 8192], P('ctx', 'tp')
The draws below stay inside these ranges and needn't reach their ends.
Inputs may be any that keep to these rules, and one draw needn't show every extreme that they name: A permutation of the positions that follow the cache: each of the values from min to max appears once. `lengths`: at least one shard is full in every draw.
All inputs are finite; a program needn't handle non-finite values.
Results may differ from the reference program's by a relative error of at most 0.015.
Values may be sent and summed in bfloat16 or wider, within the bound.
A program may use at most 128 MiB of HBM per device.

```python
import math
import jax
import jax.numpy as jnp
from jax import lax

D = 8192
QUERY_HEADS = 64
VALUE_HEADS_ALL = 8
HEAD_SIZE = 128
CACHE_DEV = 4096
CACHE_SLOTS = 65536
TURN_TOKENS = 1024
SHARDS = 16


def draw_queries(key, part):
    key = jax.random.fold_in(key, 3)
    sampled_values = jnp.clip(1.7 * jax.random.normal(key, (TURN_TOKENS, QUERY_HEADS * HEAD_SIZE), jnp.float32), -8.0, 8.0)
    return sampled_values.astype(jnp.bfloat16)


def draw_cache_keys(key, part):
    key = jax.random.fold_in(key, 5)
    sampled_values = jnp.clip(1.7 * jax.random.normal(key, (CACHE_SLOTS, VALUE_HEADS_ALL * HEAD_SIZE), jnp.float32), -8.0, 8.0)
    return sampled_values.astype(jnp.bfloat16)


def draw_positions(key, part):
    key = jax.random.fold_in(key, 7)
    return (jax.random.permutation(key, TURN_TOKENS) + CACHE_SLOTS).astype(jnp.int32)


def draw_lengths(key, part):
    key = jax.random.fold_in(key, 9)
    first_key, second_key = jax.random.split(key)
    filled = jax.random.randint(first_key, (SHARDS,), CACHE_DEV // 4, CACHE_DEV + 1)
    full_shard = jax.random.randint(second_key, (), 0, SHARDS)
    filled = jnp.where(jnp.arange(SHARDS) == full_shard, CACHE_DEV, filled)
    return filled.astype(jnp.int32)


def shard_levels(rng, extent, pieces, smallest, largest):
    loudness = 1.0
    for dim, shards_of in pieces:
        steps = jax.random.uniform(jax.random.fold_in(jax.random.fold_in(rng, 6), dim), (shards_of,), jnp.float32, smallest / len(pieces), largest / len(pieces))
        loudness = loudness * jnp.repeat(jnp.exp(steps), extent[dim] // shards_of).reshape((-1,) + (1,) * (len(extent) - 1 - dim))
    return loudness


def bell_draw(stream_key, extent, deviation, most, pieces=(), kind=jnp.bfloat16):
    array = jax.random.normal(stream_key, extent, jnp.float32) * deviation
    if len(pieces) > 0:
        array = shard_levels(stream_key, extent, pieces, -0.22, 0.18) * array
    return jnp.clip(array, min=-most, max=most).astype(kind)


def setup_inputs(seed: int = 0) -> dict:
    arg_keys = jax.random.split(jax.random.key(seed), 9)
    return {
        "queries": draw_queries(jax.random.fold_in(arg_keys[8], 71), 0),
        "cache_keys": draw_cache_keys(jax.random.fold_in(arg_keys[8], 71), 0),
        "stored_values": bell_draw(arg_keys[2], (CACHE_SLOTS, VALUE_HEADS_ALL * HEAD_SIZE), 1.0, 6.0, ((0, 16), (1, 8))),
        "fresh_keys": bell_draw(arg_keys[3], (TURN_TOKENS, VALUE_HEADS_ALL * HEAD_SIZE), 2.5, 12.0, ((0, 16), (1, 8))),
        "fresh_values": bell_draw(arg_keys[4], (TURN_TOKENS, VALUE_HEADS_ALL * HEAD_SIZE), 1.0, 6.0, ((0, 16), (1, 8))),
        "positions": draw_positions(jax.random.fold_in(arg_keys[8], 71), 0),
        "lengths": draw_lengths(jax.random.fold_in(arg_keys[8], 71), 0),
        "out_weight": bell_draw(arg_keys[7], (QUERY_HEADS * HEAD_SIZE, D), (QUERY_HEADS * HEAD_SIZE) ** -0.5, 0.0625, ((0, 8),)),
    }


def reference(queries, cache_keys, stored_values, fresh_keys, fresh_values, positions, lengths, out_weight):
    group_width = QUERY_HEADS // VALUE_HEADS_ALL
    block_size = min(128, TURN_TOKENS)
    scale_factor = 1.0 / math.sqrt(HEAD_SIZE)
    slot_index = jnp.arange(CACHE_SLOTS, dtype=jnp.int32)
    cache_valid = slot_index % CACHE_DEV < lengths[slot_index // CACHE_DEV]
    turn_valid = positions[None, :] <= positions[:, None]

    def one_head(head_index):
        kv_index = head_index // group_width
        query_head = lax.dynamic_slice_in_dim(queries, (head_index * HEAD_SIZE).astype(jnp.int32), HEAD_SIZE, 1)
        key_cache = lax.dynamic_slice_in_dim(cache_keys, (kv_index * HEAD_SIZE).astype(jnp.int32), HEAD_SIZE, 1)
        value_cache = lax.dynamic_slice_in_dim(stored_values, (kv_index * HEAD_SIZE).astype(jnp.int32), HEAD_SIZE, 1)
        key_turn = lax.dynamic_slice_in_dim(fresh_keys, (kv_index * HEAD_SIZE).astype(jnp.int32), HEAD_SIZE, 1)
        value_turn = lax.dynamic_slice_in_dim(fresh_values, (kv_index * HEAD_SIZE).astype(jnp.int32), HEAD_SIZE, 1)
        all_keys = jnp.concatenate([key_cache, key_turn], axis=0)
        all_values = jnp.concatenate([value_cache, value_turn], axis=0)

        def one_block(block_index):
            query_block = lax.dynamic_slice_in_dim(query_head, (block_index * block_size).astype(jnp.int32), block_size, 0)
            turn_block = lax.dynamic_slice_in_dim(turn_valid, (block_index * block_size).astype(jnp.int32), block_size, 0)
            valid_keys = jnp.concatenate([jnp.broadcast_to(cache_valid[None, :], (block_size, CACHE_SLOTS)), turn_block], axis=1)
            scores = jnp.dot(query_block, all_keys.T, preferred_element_type=jnp.float32) * scale_factor
            scores = jnp.where(valid_keys, scores, -1e+30)
            peak_now = lax.optimization_barrier(jnp.max(scores, axis=1, keepdims=True))
            weights = jnp.where(valid_keys, jnp.exp(scores - peak_now), 0.0)
            totals = lax.optimization_barrier(jnp.sum(weights, axis=1, keepdims=True))
            mixed_rows = jnp.dot(weights.astype(jnp.bfloat16), all_values, preferred_element_type=jnp.float32)
            return mixed_rows / totals
        blocks = lax.map(one_block, jnp.arange(TURN_TOKENS // block_size, dtype=jnp.int32))
        return blocks.reshape(TURN_TOKENS, HEAD_SIZE)
    heads = lax.map(one_head, jnp.arange(QUERY_HEADS, dtype=jnp.int32))
    attended = jnp.transpose(heads, (1, 0, 2)).reshape(TURN_TOKENS, QUERY_HEADS * HEAD_SIZE).astype(jnp.bfloat16)
    return jnp.dot(attended, out_weight, preferred_element_type=jnp.float32).astype(jnp.bfloat16)
```

```python
import functools
import math

import jax
import jax.numpy as jnp
from jax import lax
from jax.experimental import pallas as pl
from jax.experimental.pallas import tpu as pltpu
from jax.sharding import PartitionSpec as P

HEAD = 128
GROUP = 8
FRESH = 128
BLOCKS = 4
LOW = -1e30
FAR = 1e9
ONES = 16
F32 = jnp.float32
BF16 = jnp.bfloat16
UNIT = math.log2(math.e) / math.sqrt(HEAD)
MESH = pl.DeviceIdType.MESH


def kernel(
    grid_ctx,
    grid_tp,
    q_ref,
    fk_ref,
    fv_ref,
    pos_ref,
    len_ref,
    k_hbm,
    v_hbm,
    w_hbm,
    out_ref,
    qbuf,
    meta,
    kbuf,
    vbuf,
    v_raw,
    wbuf,
    s_a,
    s_b,
    f_a,
    f_b,
    peak,
    m_now,
    acc,
    m_own,
    acc_own,
    part_out,
    part_log,
    got_out,
    got_log,
    attended,
    proj_out,
    proj_got,
    local_sem,
    q_send,
    q_recv,
    meta_send,
    meta_recv,
    kv_send,
    kv_recv,
    out_send,
    out_recv,
    log_send,
    log_recv,
    proj_send,
    proj_recv,
):
    nz, ny = grid_ctx
    tz, tx = grid_tp
    peers = nz * ny
    columns = tz * tx
    tokens = q_ref.shape[0]
    rows = tokens * GROUP
    slots = k_hbm.shape[0]
    block = slots // BLOCKS

    ctx = lax.axis_index("ctx")
    tp = lax.axis_index("tp")
    core = lax.rem(ctx, 2)
    chip = lax.div(ctx, 2)
    cz, cy = lax.div(chip, ny), lax.rem(chip, ny)
    pz, px = lax.div(tp, tx), lax.rem(tp, tx)
    partner = ctx + 1 - 2 * core

    def to_chip(k):
        z = lax.rem(cz + nz - lax.div(k, ny), nz)
        y = lax.rem(cy + ny - lax.rem(k, ny), ny)
        return (z * ny + y) * 2 + core

    def from_chip(k):
        z = lax.rem(cz + lax.div(k, ny), nz)
        y = lax.rem(cy + lax.rem(k, ny), ny)
        return (z * ny + y) * 2 + core

    def to_column(k):
        z = lax.rem(pz + lax.div(k, tx), tz)
        x = lax.rem(px + lax.rem(k, tx), tx)
        return z * tx + x

    def remote(src, dst, send, recv, where):
        return pltpu.make_async_remote_copy(
            src_ref=src, dst_ref=dst, send_sem=send, recv_sem=recv, device_id=where, device_id_type=MESH
        )

    def q_copy(k):
        return remote(qbuf.at[0], qbuf.at[k], q_send.at[k], q_recv.at[k], {"ctx": to_chip(k)})

    def meta_copy(k):
        return remote(meta.at[0], meta.at[k], meta_send.at[k], meta_recv.at[k], {"ctx": to_chip(k)})

    def meta_partner():
        return remote(meta.at[0], meta.at[peers], meta_send.at[peers], meta_recv.at[peers], {"ctx": partner})

    def k_partner():
        return remote(kbuf.at[0], kbuf.at[1], kv_send.at[0], kv_recv.at[0], {"ctx": partner})

    def v_partner():
        return remote(vbuf.at[0], vbuf.at[1], kv_send.at[1], kv_recv.at[1], {"ctx": partner})

    def out_copy(k):
        return remote(part_out.at[k], got_out.at[k], out_send.at[k], out_recv.at[k], {"ctx": from_chip(k)})

    def log_copy(k):
        return remote(part_log.at[k], got_log.at[k], log_send.at[k], log_recv.at[k], {"ctx": from_chip(k)})

    def proj_copy(k):
        return remote(proj_out.at[k], proj_got.at[k], proj_send.at[k], proj_recv.at[k], {"tp": to_column(k)})

    k_load = pltpu.make_async_copy(k_hbm, kbuf.at[0, pl.ds(0, slots)], local_sem.at[0])
    v_load = pltpu.make_async_copy(v_hbm, v_raw, local_sem.at[1])
    w_load = pltpu.make_async_copy(w_hbm, wbuf, local_sem.at[2])
    k_load.start()
    v_load.start()

    barrier = pltpu.get_barrier_semaphore()
    for k in range(1, peers):
        pl.semaphore_signal(barrier, inc=1, device_id={"ctx": to_chip(k)}, device_id_type=MESH)
    pl.semaphore_signal(barrier, inc=1, device_id={"ctx": partner}, device_id_type=MESH)
    for k in range(1, columns):
        pl.semaphore_signal(barrier, inc=1, device_id={"tp": to_column(k)}, device_id_type=MESH)

    stacked = jnp.concatenate([q_ref[:, h * HEAD : (h + 1) * HEAD].astype(F32) for h in range(GROUP)], axis=0)
    qbuf[0] = stacked.T.astype(BF16)
    meta[0] = jnp.broadcast_to(jnp.concatenate([pos_ref[...].astype(F32)] * GROUP, axis=1), (8, rows))
    spare = jnp.zeros((FRESH - tokens, HEAD), F32)
    kbuf[0, pl.ds(slots, FRESH), :] = jnp.concatenate([fk_ref[...].astype(F32), spare], axis=0).astype(BF16)
    vbuf[0, pl.ds(0, HEAD), pl.ds(slots, FRESH)] = (
        jnp.concatenate([fv_ref[...].astype(F32), spare], axis=0).T.astype(BF16)
    )
    vbuf[0, pl.ds(HEAD, ONES), pl.ds(slots, FRESH)] = jnp.ones((ONES, FRESH), BF16)

    pl.semaphore_wait(barrier, peers - 1 + 1 + columns - 1)
    first_sends = min(4, peers)
    for k in range(1, first_sends):
        q_copy(k).start()
    for k in range(1, peers):
        meta_copy(k).start()
    meta_partner().start()

    filled = len_ref[0]
    k_load.wait()
    lead = kbuf[0, pl.ds(0, 16), :].astype(F32)[0:1]
    tidy = block // 2

    @pl.loop(0, slots // tidy)
    def _(c):
        at = pl.ds(pl.multiple_of(c * tidy, tidy), tidy)
        valid = lax.broadcasted_iota(jnp.int32, (tidy, HEAD), 0) + c * tidy < filled
        kbuf[0, at, :] = jnp.where(valid, kbuf[0, at, :].astype(F32), lead).astype(BF16)

    k_partner().start()
    v_load.wait()

    @pl.loop(0, slots // tidy)
    def _(c):
        at = pl.ds(pl.multiple_of(c * tidy, tidy), tidy)
        valid = lax.broadcasted_iota(jnp.int32, (HEAD, tidy), 1) + c * tidy < filled
        vbuf[0, pl.ds(0, HEAD), at] = jnp.where(valid, v_raw[at, :].astype(F32).T, 0.0).astype(BF16)
        vbuf[0, pl.ds(HEAD, ONES), at] = jnp.where(valid[:ONES], 1.0, 0.0).astype(BF16)

    v_partner().start()
    w_load.start()

    def fresh_scores(tile, shard, fresh):
        row = lax.broadcasted_iota(jnp.int32, (FRESH, FRESH), 0)
        lane = lax.broadcasted_iota(jnp.int32, (FRESH, FRESH), 1)
        spots = jnp.where(row == lane, meta[shard * peers, 0:1, pl.ds(0, FRESH)], 0.0)
        spot = jnp.where(row[:, :1] < tokens, jnp.sum(spots, axis=1, keepdims=True), FAR)
        s = jnp.dot(kbuf[shard, pl.ds(slots, FRESH), :], qbuf[tile], preferred_element_type=F32)
        s = jnp.where(spot <= meta[tile, 0:1, :], s, LOW)
        fresh[...] = s
        return s

    wide = min(256, block)

    def top_of(s):
        return jnp.max(s.reshape(s.shape[0] // 8, 8, rows), axis=0)

    def phase(now, then, tile, shard_now, shard_then):
        if now is not None:
            s_now, f_now = now
            m_old = m_now[0:1, :]
            m_new = jnp.maximum(m_old, jnp.max(peak[...], axis=0, keepdims=True))
            fade = jnp.exp2((m_old - m_new) * UNIT)
            m_now[...] = jnp.broadcast_to(m_new, (8, rows))
            mk = m_new * UNIT
            p = jnp.exp2(f_now[...] * UNIT - mk).astype(BF16)
            add = jnp.dot(vbuf[shard_now, :, pl.ds(slots, FRESH)], p, preferred_element_type=F32)
            acc[...] = acc[...] * fade + add
        if then is not None:
            s_then, f_then = then
            top = top_of(fresh_scores(tile, shard_then, f_then))
        for b in range(BLOCKS):
            weights = []
            for c in range(block // wide):
                start = b * block + c * wide
                if then is not None:
                    s = jnp.dot(kbuf[shard_then, pl.ds(start, wide), :], qbuf[tile], preferred_element_type=F32)
                    s_then[pl.ds(start, wide), :] = s
                    top = jnp.maximum(top, top_of(s))
                if now is not None:
                    weights.append(jnp.exp2(s_now[pl.ds(start, wide), :] * UNIT - mk).astype(BF16))
            if now is not None:
                acc[...] += jnp.dot(
                    vbuf[shard_now, :, pl.ds(b * block, block)],
                    jnp.concatenate(weights, axis=0),
                    preferred_element_type=F32,
                )
        if then is not None:
            peak[...] = top

    def clear():
        acc[...] = jnp.zeros_like(acc)
        m_now[...] = jnp.full_like(m_now, LOW)

    def finish(k):
        total = acc[pl.ds(HEAD, 8), :]
        part_out[k] = (acc[pl.ds(0, HEAD), :] / total[0:1]).astype(BF16)
        part_log[k] = m_now[...] * UNIT + jnp.log(total) * math.log2(math.e)

    a, b = (s_a, f_a), (s_b, f_b)
    clear()
    phase(None, a, 0, None, 0)

    @pl.loop(0, peers)
    def _(t):
        shard = lax.rem(t, 2)
        tile = lax.rem(t + 1, peers)

        @pl.when(t + first_sends < peers)
        def _():
            q_copy(t + first_sends).start()

        @pl.when(t + 1 < peers)
        def _():
            q_copy(t + 1).wait_recv()
            meta_copy(t + 1).wait_recv()

        phase(a, b, tile, shard, shard)

        @pl.when(t == 0)
        def _():
            acc_own[...] = acc[...]
            m_own[...] = m_now[...]
            meta_partner().wait_recv()
            k_partner().wait_recv()

        @pl.when(t > 0)
        def _():
            finish(t)
            out_copy(t).start()
            log_copy(t).start()

        @pl.when(t + 1 < peers)
        def _():
            clear()
            phase(b, a, tile, shard, 1 - shard)

        @pl.when(t == 0)
        def _():
            v_partner().wait_recv()

        @pl.when(t + 1 == peers)
        def _():
            acc[...] = acc_own[...]
            m_now[...] = m_own[...]
            phase(b, None, None, shard, None)
            finish(0)

    for k in range(1, peers):
        out_copy(k).wait_recv()
        log_copy(k).wait_recv()
    logs = [part_log[0]] + [got_log[k] for k in range(1, peers)]
    top = functools.reduce(jnp.maximum, logs)
    shares = [jnp.exp2(log - top) for log in logs]
    whole = functools.reduce(jnp.add, shares)
    shares = [share / whole for share in shares]
    mixed = shares[0][0:1] * part_out[0].astype(F32)
    for k in range(1, peers):
        mixed += shares[k][0:1] * got_out[k].astype(F32)
    mixed = mixed.T.astype(BF16)
    for h in range(GROUP):
        attended[:, pl.ds(h * HEAD, HEAD)] = mixed[h * tokens : (h + 1) * tokens]

    w_load.wait()
    span = wbuf.shape[1] // columns

    def project(k):
        at = pl.ds(pl.multiple_of(to_column(k) * span, span), span)
        return jnp.dot(attended[...], wbuf[:, at], preferred_element_type=F32)

    @pl.loop(0, columns - 1)
    def _(s):
        k = columns - 1 - s
        proj_out[k] = project(k).astype(BF16)
        proj_copy(k).start()

    result = project(0)
    for k in range(columns - 1, 0, -1):
        proj_copy(k).wait_recv()
        result += proj_got[k].astype(F32)
    out_ref[...] = result.astype(BF16)

    for k in range(1, peers):
        q_copy(k).wait_send()
        meta_copy(k).wait_send()
        out_copy(k).wait_send()
        log_copy(k).wait_send()
    meta_partner().wait_send()
    k_partner().wait_send()
    v_partner().wait_send()
    for k in range(1, columns):
        proj_copy(k).wait_send()


def grid_of(count):
    return (2, count // 2) if count > 2 else (1, count)


def per_device(queries, cache_keys, stored_values, fresh_keys, fresh_values, positions, lengths, out_weight, sizes):
    ctx_size, tp_size = sizes
    grid_ctx, grid_tp = grid_of(ctx_size // 2), grid_of(tp_size)
    peers = ctx_size // 2
    tokens, width = queries.shape
    rows = tokens * GROUP
    slots = cache_keys.shape[0]
    span = out_weight.shape[1] // tp_size
    vmem = pl.BlockSpec(memory_space=pltpu.VMEM)
    anywhere = pl.BlockSpec(memory_space=pl.ANY)
    dma = pltpu.SemaphoreType.DMA
    return pl.pallas_call(
        functools.partial(kernel, grid_ctx, grid_tp),
        out_shape=jax.ShapeDtypeStruct((tokens, span), BF16),
        in_specs=[vmem, vmem, vmem, vmem, pl.BlockSpec(memory_space=pltpu.SMEM), anywhere, anywhere, anywhere],
        out_specs=vmem,
        scratch_shapes=[
            pltpu.VMEM((peers, HEAD, rows), BF16),
            pltpu.VMEM((peers + 1, 8, rows), F32),
            pltpu.VMEM((2, slots + FRESH, HEAD), BF16),
            pltpu.VMEM((2, HEAD + ONES, slots + FRESH), BF16),
            pltpu.VMEM((slots, HEAD), BF16),
            pltpu.VMEM(out_weight.shape, BF16),
            pltpu.VMEM((slots, rows), F32),
            pltpu.VMEM((slots, rows), F32),
            pltpu.VMEM((FRESH, rows), F32),
            pltpu.VMEM((FRESH, rows), F32),
            pltpu.VMEM((8, rows), F32),
            pltpu.VMEM((8, rows), F32),
            pltpu.VMEM((HEAD + ONES, rows), F32),
            pltpu.VMEM((8, rows), F32),
            pltpu.VMEM((HEAD + ONES, rows), F32),
            pltpu.VMEM((peers, HEAD, rows), BF16),
            pltpu.VMEM((peers, 8, rows), F32),
            pltpu.VMEM((peers, HEAD, rows), BF16),
            pltpu.VMEM((peers, 8, rows), F32),
            pltpu.VMEM((tokens, width), BF16),
            pltpu.VMEM((tp_size, tokens, span), BF16),
            pltpu.VMEM((tp_size, tokens, span), BF16),
            dma((3,)),
            dma((peers,)),
            dma((peers,)),
            dma((peers + 1,)),
            dma((peers + 1,)),
            dma((2,)),
            dma((2,)),
            dma((peers,)),
            dma((peers,)),
            dma((peers,)),
            dma((peers,)),
            dma((tp_size,)),
            dma((tp_size,)),
        ],
        compiler_params=pltpu.CompilerParams(
            collective_id=0, has_side_effects=True, vmem_limit_bytes=60 * 1024 * 1024
        ),
        cost_estimate=pl.CostEstimate(
            flops=4 * peers * rows * 2 * (slots + FRESH) * HEAD + 2 * tokens * width * out_weight.shape[1],
            bytes_accessed=2 * (out_weight.size + 2 * cache_keys.size),
            transcendentals=peers * rows * 2 * (slots + FRESH),
        ),
    )(
        queries,
        fresh_keys,
        fresh_values,
        positions.reshape(1, tokens),
        lengths,
        cache_keys,
        stored_values,
        out_weight,
    )


def solution(mesh):
    placed = (
        P("ctx", "tp"),
        P("ctx", "tp"),
        P("ctx", "tp"),
        P("ctx", "tp"),
        P("ctx", "tp"),
        P("ctx"),
        P("ctx"),
        P("tp", None),
    )
    sizes = (mesh.shape["ctx"], mesh.shape["tp"])
    return jax.shard_map(
        functools.partial(per_device, sizes=sizes),
        mesh=mesh,
        in_specs=placed,
        out_specs=P("ctx", "tp"),
        check_vma=False,
    )
```

```python
import functools
import math

import jax
import jax.numpy as jnp
from jax import lax
from jax.experimental import pallas as pl
from jax.experimental.pallas import tpu as pltpu
from jax.sharding import PartitionSpec as P

HEAD = 128
GROUP = 8
FRESH = 128
BLOCKS = 4
LOW = -1e30
FAR = 1e9
ONES = 16
F32 = jnp.float32
BF16 = jnp.bfloat16
UNIT = math.log2(math.e) / math.sqrt(HEAD)
MESH = pl.DeviceIdType.MESH


def kernel(
    grid_ctx,
    grid_tp,
    q_ref,
    fk_ref,
    fv_ref,
    pos_ref,
    len_ref,
    k_hbm,
    v_hbm,
    w_hbm,
    out_ref,
    qbuf,
    meta,
    kbuf,
    vbuf,
    v_raw,
    wbuf,
    s_a,
    s_b,
    f_a,
    f_b,
    peak,
    m_now,
    acc,
    m_own,
    acc_own,
    part_out,
    part_log,
    got_out,
    got_log,
    attended,
    proj_out,
    proj_got,
    local_sem,
    q_send,
    q_recv,
    meta_send,
    meta_recv,
    kv_send,
    kv_recv,
    out_send,
    out_recv,
    log_send,
    log_recv,
    proj_send,
    proj_recv,
):
    nz, ny = grid_ctx
    tz, tx = grid_tp
    peers = nz * ny
    columns = tz * tx
    tokens = q_ref.shape[0]
    rows = tokens * GROUP
    slots = k_hbm.shape[0]
    block = slots // BLOCKS

    ctx = lax.axis_index("ctx")
    tp = lax.axis_index("tp")
    core = lax.rem(ctx, 2)
    chip = lax.div(ctx, 2)
    cz, cy = lax.div(chip, ny), lax.rem(chip, ny)
    pz, px = lax.div(tp, tx), lax.rem(tp, tx)
    partner = ctx + 1 - 2 * core

    def to_chip(k):
        z = lax.rem(cz + nz - lax.div(k, ny), nz)
        y = lax.rem(cy + ny - lax.rem(k, ny), ny)
        return (z * ny + y) * 2 + core

    def from_chip(k):
        z = lax.rem(cz + lax.div(k, ny), nz)
        y = lax.rem(cy + lax.rem(k, ny), ny)
        return (z * ny + y) * 2 + core

    def to_column(k):
        z = lax.rem(pz + lax.div(k, tx), tz)
        x = lax.rem(px + lax.rem(k, tx), tx)
        return z * tx + x

    def remote(src, dst, send, recv, where):
        return pltpu.make_async_remote_copy(
            src_ref=src, dst_ref=dst, send_sem=send, recv_sem=recv, device_id=where, device_id_type=MESH
        )

    def q_copy(k):
        return remote(qbuf.at[0], qbuf.at[k], q_send.at[k], q_recv.at[k], {"ctx": to_chip(k)})

    def meta_copy(k):
        return remote(meta.at[0], meta.at[k], meta_send.at[k], meta_recv.at[k], {"ctx": to_chip(k)})

    def meta_partner():
        return remote(meta.at[0], meta.at[peers], meta_send.at[peers], meta_recv.at[peers], {"ctx": partner})

    def k_partner():
        return remote(kbuf.at[0], kbuf.at[1], kv_send.at[0], kv_recv.at[0], {"ctx": partner})

    def v_partner():
        return remote(vbuf.at[0], vbuf.at[1], kv_send.at[1], kv_recv.at[1], {"ctx": partner})

    def out_copy(k):
        return remote(part_out.at[k], got_out.at[k], out_send.at[k], out_recv.at[k], {"ctx": from_chip(k)})

    def log_copy(k):
        return remote(part_log.at[k], got_log.at[k], log_send.at[k], log_recv.at[k], {"ctx": from_chip(k)})

    def proj_copy(k):
        return remote(proj_out.at[k], proj_got.at[k], proj_send.at[k], proj_recv.at[k], {"tp": to_column(k)})

    k_load = pltpu.make_async_copy(k_hbm, kbuf.at[0, pl.ds(0, slots)], local_sem.at[0])
    v_load = pltpu.make_async_copy(v_hbm, v_raw, local_sem.at[1])
    w_load = pltpu.make_async_copy(w_hbm, wbuf, local_sem.at[2])
    k_load.start()
    v_load.start()

    barrier = pltpu.get_barrier_semaphore()
    for k in range(1, peers):
        pl.semaphore_signal(barrier, inc=1, device_id={"ctx": to_chip(k)}, device_id_type=MESH)
    pl.semaphore_signal(barrier, inc=1, device_id={"ctx": partner}, device_id_type=MESH)
    for k in range(1, columns):
        pl.semaphore_signal(barrier, inc=1, device_id={"tp": to_column(k)}, device_id_type=MESH)

    stacked = jnp.concatenate([q_ref[:, h * HEAD : (h + 1) * HEAD].astype(F32) for h in range(GROUP)], axis=0)
    qbuf[0] = stacked.T.astype(BF16)
    meta[0] = jnp.broadcast_to(jnp.concatenate([pos_ref[...].astype(F32)] * GROUP, axis=1), (8, rows))
    spare = jnp.zeros((FRESH - tokens, HEAD), F32)
    kbuf[0, pl.ds(slots, FRESH), :] = jnp.concatenate([fk_ref[...].astype(F32), spare], axis=0).astype(BF16)
    vbuf[0, pl.ds(0, HEAD), pl.ds(slots, FRESH)] = (
        jnp.concatenate([fv_ref[...].astype(F32), spare], axis=0).T.astype(BF16)
    )
    vbuf[0, pl.ds(HEAD, ONES), pl.ds(slots, FRESH)] = jnp.ones((ONES, FRESH), BF16)

    pl.semaphore_wait(barrier, peers - 1 + 1 + columns - 1)
    first_sends = min(4, peers)
    for k in range(1, first_sends):
        q_copy(k).start()
    for k in range(1, peers):
        meta_copy(k).start()
    meta_partner().start()

    filled = len_ref[0]
    k_load.wait()
    lead = kbuf[0, pl.ds(0, 16), :].astype(F32)[0:1]
    tidy = block // 2

    @pl.loop(0, slots // tidy)
    def _(c):
        at = pl.ds(pl.multiple_of(c * tidy, tidy), tidy)
        valid = lax.broadcasted_iota(jnp.int32, (tidy, HEAD), 0) + c * tidy < filled
        kbuf[0, at, :] = jnp.where(valid, kbuf[0, at, :].astype(F32), lead).astype(BF16)

    k_partner().start()
    v_load.wait()

    @pl.loop(0, slots // tidy)
    def _(c):
        at = pl.ds(pl.multiple_of(c * tidy, tidy), tidy)
        valid = lax.broadcasted_iota(jnp.int32, (HEAD, tidy), 1) + c * tidy < filled
        vbuf[0, pl.ds(0, HEAD), at] = jnp.where(valid, v_raw[at, :].astype(F32).T, 0.0).astype(BF16)
        vbuf[0, pl.ds(HEAD, ONES), at] = jnp.where(valid[:ONES], 1.0, 0.0).astype(BF16)

    v_partner().start()
    w_load.start()

    def fresh_scores(tile, shard, fresh):
        row = lax.broadcasted_iota(jnp.int32, (FRESH, FRESH), 0)
        lane = lax.broadcasted_iota(jnp.int32, (FRESH, FRESH), 1)
        spots = jnp.where(row == lane, meta[shard * peers, 0:1, pl.ds(0, FRESH)], 0.0)
        spot = jnp.where(row[:, :1] < tokens, jnp.sum(spots, axis=1, keepdims=True), FAR)
        s = jnp.dot(kbuf[shard, pl.ds(slots, FRESH), :], qbuf[tile], preferred_element_type=F32)
        s = jnp.where(spot <= meta[tile, 0:1, :], s, LOW)
        fresh[...] = s
        return s

    wide = min(1024, block)

    def top_of(s):
        return jnp.max(s.reshape(s.shape[0] // 8, 8, rows), axis=0)

    def phase(now, then, tile, shard_now, shard_then):
        if now is not None:
            s_now, f_now = now
            m_old = m_now[0:1, :]
            m_new = jnp.maximum(m_old, jnp.max(peak[...], axis=0, keepdims=True))
            fade = jnp.exp2((m_old - m_new) * UNIT)
            m_now[...] = jnp.broadcast_to(m_new, (8, rows))
            mk = m_new * UNIT
            p = jnp.exp2(f_now[...] * UNIT - mk).astype(BF16)
            add = jnp.dot(vbuf[shard_now, :, pl.ds(slots, FRESH)], p, preferred_element_type=F32)
            acc[...] = acc[...] * fade + add
        if then is not None:
            s_then, f_then = then
            top = top_of(fresh_scores(tile, shard_then, f_then))
        for b in range(BLOCKS):
            weights = []
            for c in range(block // wide):
                start = b * block + c * wide
                if then is not None:
                    s = jnp.dot(kbuf[shard_then, pl.ds(start, wide), :], qbuf[tile], preferred_element_type=F32)
                    s_then[pl.ds(start, wide), :] = s
                    top = jnp.maximum(top, top_of(s))
                if now is not None:
                    weights.append(jnp.exp2(s_now[pl.ds(start, wide), :] * UNIT - mk).astype(BF16))
            if now is not None:
                acc[...] += jnp.dot(
                    vbuf[shard_now, :, pl.ds(b * block, block)],
                    jnp.concatenate(weights, axis=0),
                    preferred_element_type=F32,
                )
        if then is not None:
            peak[...] = top

    def clear():
        acc[...] = jnp.zeros_like(acc)
        m_now[...] = jnp.full_like(m_now, LOW)

    def finish(k):
        total = acc[pl.ds(HEAD, 8), :]
        part_out[k] = (acc[pl.ds(0, HEAD), :] / total[0:1]).astype(BF16)
        part_log[k] = m_now[...] * UNIT + jnp.log(total) * math.log2(math.e)

    a, b = (s_a, f_a), (s_b, f_b)
    clear()
    phase(None, a, 0, None, 0)

    @pl.loop(0, peers)
    def _(t):
        shard = lax.rem(t, 2)
        tile = lax.rem(t + 1, peers)

        @pl.when(t + first_sends < peers)
        def _():
            q_copy(t + first_sends).start()

        @pl.when(t + 1 < peers)
        def _():
            q_copy(t + 1).wait_recv()
            meta_copy(t + 1).wait_recv()

        phase(a, b, tile, shard, shard)

        @pl.when(t == 0)
        def _():
            acc_own[...] = acc[...]
            m_own[...] = m_now[...]
            meta_partner().wait_recv()
            k_partner().wait_recv()

        @pl.when(t > 0)
        def _():
            finish(t)
            out_copy(t).start()
            log_copy(t).start()

        @pl.when(t + 1 < peers)
        def _():
            clear()
            phase(b, a, tile, shard, 1 - shard)

        @pl.when(t == 0)
        def _():
            v_partner().wait_recv()

        @pl.when(t + 1 == peers)
        def _():
            acc[...] = acc_own[...]
            m_now[...] = m_own[...]
            phase(b, None, None, shard, None)
            finish(0)

    for k in range(1, peers):
        out_copy(k).wait_recv()
        log_copy(k).wait_recv()
    logs = [part_log[0]] + [got_log[k] for k in range(1, peers)]
    top = functools.reduce(jnp.maximum, logs)
    shares = [jnp.exp2(log - top) for log in logs]
    whole = functools.reduce(jnp.add, shares)
    shares = [share / whole for share in shares]
    mixed = shares[0][0:1] * part_out[0].astype(F32)
    for k in range(1, peers):
        mixed += shares[k][0:1] * got_out[k].astype(F32)
    mixed = mixed.T.astype(BF16)
    for h in range(GROUP):
        attended[:, pl.ds(h * HEAD, HEAD)] = mixed[h * tokens : (h + 1) * tokens]

    w_load.wait()
    span = wbuf.shape[1] // columns

    def project(k):
        at = pl.ds(pl.multiple_of(to_column(k) * span, span), span)
        return jnp.dot(attended[...], wbuf[:, at], preferred_element_type=F32)

    @pl.loop(0, columns - 1)
    def _(s):
        k = columns - 1 - s
        proj_out[k] = project(k).astype(BF16)
        proj_copy(k).start()

    result = project(0)
    for k in range(columns - 1, 0, -1):
        proj_copy(k).wait_recv()
        result += proj_got[k].astype(F32)
    out_ref[...] = result.astype(BF16)

    for k in range(1, peers):
        q_copy(k).wait_send()
        meta_copy(k).wait_send()
        out_copy(k).wait_send()
        log_copy(k).wait_send()
    meta_partner().wait_send()
    k_partner().wait_send()
    v_partner().wait_send()
    for k in range(1, columns):
        proj_copy(k).wait_send()


def grid_of(count):
    return (2, count // 2) if count > 2 else (1, count)


def per_device(queries, cache_keys, stored_values, fresh_keys, fresh_values, positions, lengths, out_weight, sizes):
    ctx_size, tp_size = sizes
    grid_ctx, grid_tp = grid_of(ctx_size // 2), grid_of(tp_size)
    peers = ctx_size // 2
    tokens, width = queries.shape
    rows = tokens * GROUP
    slots = cache_keys.shape[0]
    span = out_weight.shape[1] // tp_size
    vmem = pl.BlockSpec(memory_space=pltpu.VMEM)
    anywhere = pl.BlockSpec(memory_space=pl.ANY)
    dma = pltpu.SemaphoreType.DMA
    return pl.pallas_call(
        functools.partial(kernel, grid_ctx, grid_tp),
        out_shape=jax.ShapeDtypeStruct((tokens, span), BF16),
        in_specs=[vmem, vmem, vmem, vmem, pl.BlockSpec(memory_space=pltpu.SMEM), anywhere, anywhere, anywhere],
        out_specs=vmem,
        scratch_shapes=[
            pltpu.VMEM((peers, HEAD, rows), BF16),
            pltpu.VMEM((peers + 1, 8, rows), F32),
            pltpu.VMEM((2, slots + FRESH, HEAD), BF16),
            pltpu.VMEM((2, HEAD + ONES, slots + FRESH), BF16),
            pltpu.VMEM((slots, HEAD), BF16),
            pltpu.VMEM(out_weight.shape, BF16),
            pltpu.VMEM((slots, rows), F32),
            pltpu.VMEM((slots, rows), F32),
            pltpu.VMEM((FRESH, rows), F32),
            pltpu.VMEM((FRESH, rows), F32),
            pltpu.VMEM((8, rows), F32),
            pltpu.VMEM((8, rows), F32),
            pltpu.VMEM((HEAD + ONES, rows), F32),
            pltpu.VMEM((8, rows), F32),
            pltpu.VMEM((HEAD + ONES, rows), F32),
            pltpu.VMEM((peers, HEAD, rows), BF16),
            pltpu.VMEM((peers, 8, rows), F32),
            pltpu.VMEM((peers, HEAD, rows), BF16),
            pltpu.VMEM((peers, 8, rows), F32),
            pltpu.VMEM((tokens, width), BF16),
            pltpu.VMEM((tp_size, tokens, span), BF16),
            pltpu.VMEM((tp_size, tokens, span), BF16),
            dma((3,)),
            dma((peers,)),
            dma((peers,)),
            dma((peers + 1,)),
            dma((peers + 1,)),
            dma((2,)),
            dma((2,)),
            dma((peers,)),
            dma((peers,)),
            dma((peers,)),
            dma((peers,)),
            dma((tp_size,)),
            dma((tp_size,)),
        ],
        compiler_params=pltpu.CompilerParams(
            collective_id=0, has_side_effects=True, vmem_limit_bytes=60 * 1024 * 1024
        ),
        cost_estimate=pl.CostEstimate(
            flops=4 * peers * rows * 2 * (slots + FRESH) * HEAD + 2 * tokens * width * out_weight.shape[1],
            bytes_accessed=2 * (out_weight.size + 2 * cache_keys.size),
            transcendentals=peers * rows * 2 * (slots + FRESH),
        ),
    )(
        queries,
        fresh_keys,
        fresh_values,
        positions.reshape(1, tokens),
        lengths,
        cache_keys,
        stored_values,
        out_weight,
    )


def solution(mesh):
    placed = (
        P("ctx", "tp"),
        P("ctx", "tp"),
        P("ctx", "tp"),
        P("ctx", "tp"),
        P("ctx", "tp"),
        P("ctx"),
        P("ctx"),
        P("tp", None),
    )
    sizes = (mesh.shape["ctx"], mesh.shape["tp"])
    return jax.shard_map(
        functools.partial(per_device, sizes=sizes),
        mesh=mesh,
        in_specs=placed,
        out_specs=P("ctx", "tp"),
        check_vma=False,
    )
```

```python
import functools
import math

import jax
import jax.numpy as jnp
from jax import lax
from jax.experimental import pallas as pl
from jax.experimental.pallas import tpu as pltpu
from jax.sharding import PartitionSpec as P

HEAD = 128
GROUP = 8
FRESH = 128
BLOCKS = 4
LOW = -1e30
FAR = 1e9
ONES = 16
F32 = jnp.float32
BF16 = jnp.bfloat16
UNIT = math.log2(math.e) / math.sqrt(HEAD)
MESH = pl.DeviceIdType.MESH


def kernel(
    grid_ctx,
    grid_tp,
    q_ref,
    fk_ref,
    fv_ref,
    pos_ref,
    len_ref,
    k_hbm,
    v_hbm,
    w_hbm,
    out_ref,
    qbuf,
    q_two,
    meta,
    kbuf,
    vbuf,
    v_raw,
    wbuf,
    s_a,
    s_b,
    f_a,
    f_b,
    peak,
    m_now,
    acc,
    m_own,
    acc_own,
    part_out,
    part_log,
    got_out,
    got_log,
    attended,
    proj_out,
    proj_got,
    local_sem,
    q_send,
    q_recv,
    meta_send,
    meta_recv,
    kv_send,
    kv_recv,
    out_send,
    out_recv,
    log_send,
    log_recv,
    proj_send,
    proj_recv,
):
    nz, ny = grid_ctx
    tz, tx = grid_tp
    peers = nz * ny
    columns = tz * tx
    tokens = q_ref.shape[0]
    rows = tokens * GROUP
    slots = k_hbm.shape[0]
    block = slots // BLOCKS

    ctx = lax.axis_index("ctx")
    tp = lax.axis_index("tp")
    core = lax.rem(ctx, 2)
    chip = lax.div(ctx, 2)
    cz, cy = lax.div(chip, ny), lax.rem(chip, ny)
    pz, px = lax.div(tp, tx), lax.rem(tp, tx)
    partner = ctx + 1 - 2 * core

    def to_chip(k):
        z = lax.rem(cz + nz - lax.div(k, ny), nz)
        y = lax.rem(cy + ny - lax.rem(k, ny), ny)
        return (z * ny + y) * 2 + core

    def from_chip(k):
        z = lax.rem(cz + lax.div(k, ny), nz)
        y = lax.rem(cy + lax.rem(k, ny), ny)
        return (z * ny + y) * 2 + core

    def to_column(k):
        z = lax.rem(pz + lax.div(k, tx), tz)
        x = lax.rem(px + lax.rem(k, tx), tx)
        return z * tx + x

    def remote(src, dst, send, recv, where):
        return pltpu.make_async_remote_copy(
            src_ref=src, dst_ref=dst, send_sem=send, recv_sem=recv, device_id=where, device_id_type=MESH
        )

    def q_copy(k):
        return remote(qbuf.at[0], qbuf.at[k], q_send.at[k], q_recv.at[k], {"ctx": to_chip(k)})

    def meta_copy(k):
        return remote(meta.at[0], meta.at[k], meta_send.at[k], meta_recv.at[k], {"ctx": to_chip(k)})

    def meta_partner():
        return remote(meta.at[0], meta.at[peers], meta_send.at[peers], meta_recv.at[peers], {"ctx": partner})

    def k_partner():
        return remote(kbuf.at[0], kbuf.at[1], kv_send.at[0], kv_recv.at[0], {"ctx": partner})

    def v_partner():
        return remote(vbuf.at[0], vbuf.at[1], kv_send.at[1], kv_recv.at[1], {"ctx": partner})

    def out_copy(k):
        return remote(part_out.at[k], got_out.at[k], out_send.at[k], out_recv.at[k], {"ctx": from_chip(k)})

    def log_copy(k):
        return remote(part_log.at[k], got_log.at[k], log_send.at[k], log_recv.at[k], {"ctx": from_chip(k)})

    def proj_copy(k):
        return remote(proj_out.at[k], proj_got.at[k], proj_send.at[k], proj_recv.at[k], {"tp": to_column(k)})

    k_load = pltpu.make_async_copy(k_hbm, kbuf.at[0, pl.ds(0, slots), pl.ds(0, HEAD)], local_sem.at[0])
    v_load = pltpu.make_async_copy(v_hbm, v_raw, local_sem.at[1])
    w_load = pltpu.make_async_copy(w_hbm, wbuf, local_sem.at[2])
    k_load.start()
    v_load.start()

    barrier = pltpu.get_barrier_semaphore()
    for k in range(1, peers):
        pl.semaphore_signal(barrier, inc=1, device_id={"ctx": to_chip(k)}, device_id_type=MESH)
    pl.semaphore_signal(barrier, inc=1, device_id={"ctx": partner}, device_id_type=MESH)
    for k in range(1, columns):
        pl.semaphore_signal(barrier, inc=1, device_id={"tp": to_column(k)}, device_id_type=MESH)

    stacked = jnp.concatenate([q_ref[:, h * HEAD : (h + 1) * HEAD].astype(F32) for h in range(GROUP)], axis=0)
    qbuf[0] = stacked.T.astype(BF16)
    meta[0] = jnp.broadcast_to(jnp.concatenate([pos_ref[...].astype(F32)] * GROUP, axis=1), (8, rows))
    spare = jnp.zeros((FRESH - tokens, HEAD), F32)
    fresh_keys = jnp.concatenate([fk_ref[...].astype(F32), spare], axis=0).astype(BF16)
    for half in range(2):
        kbuf[0, pl.ds(slots, FRESH), pl.ds(half * HEAD, HEAD)] = fresh_keys
    vbuf[0, pl.ds(0, HEAD), pl.ds(slots, FRESH)] = (
        jnp.concatenate([fv_ref[...].astype(F32), spare], axis=0).T.astype(BF16)
    )
    vbuf[0, pl.ds(HEAD, ONES), pl.ds(slots, FRESH)] = jnp.ones((ONES, FRESH), BF16)

    pl.semaphore_wait(barrier, peers - 1 + 1 + columns - 1)
    first_sends = min(4, peers)
    for k in range(1, first_sends):
        q_copy(k).start()
    for k in range(1, peers):
        meta_copy(k).start()
    meta_partner().start()

    filled = len_ref[0]
    k_load.wait()
    lead = kbuf[0, pl.ds(0, 16), pl.ds(0, HEAD)].astype(F32)[0:1]
    tidy = block // 2

    @pl.loop(0, slots // tidy)
    def _(c):
        at = pl.ds(pl.multiple_of(c * tidy, tidy), tidy)
        valid = lax.broadcasted_iota(jnp.int32, (tidy, HEAD), 0) + c * tidy < filled
        keys = jnp.where(valid, kbuf[0, at, pl.ds(0, HEAD)].astype(F32), lead).astype(BF16)
        kbuf[0, at, pl.ds(0, HEAD)] = keys
        kbuf[0, at, pl.ds(HEAD, HEAD)] = keys

    k_partner().start()
    v_load.wait()

    @pl.loop(0, slots // tidy)
    def _(c):
        at = pl.ds(pl.multiple_of(c * tidy, tidy), tidy)
        valid = lax.broadcasted_iota(jnp.int32, (HEAD, tidy), 1) + c * tidy < filled
        vbuf[0, pl.ds(0, HEAD), at] = jnp.where(valid, v_raw[at, :].astype(F32).T, 0.0).astype(BF16)
        vbuf[0, pl.ds(HEAD, ONES), at] = jnp.where(valid[:ONES], 1.0, 0.0).astype(BF16)

    v_partner().start()
    w_load.start()

    def split_queries(tile):
        scaled = qbuf[tile].astype(F32) * UNIT
        high = scaled.astype(BF16)
        q_two[pl.ds(0, HEAD), :] = high
        q_two[pl.ds(HEAD, HEAD), :] = (scaled - high.astype(F32)).astype(BF16)

    def fresh_scores(tile, shard, fresh):
        row = lax.broadcasted_iota(jnp.int32, (FRESH, FRESH), 0)
        lane = lax.broadcasted_iota(jnp.int32, (FRESH, FRESH), 1)
        spots = jnp.where(row == lane, meta[shard * peers, 0:1, pl.ds(0, FRESH)], 0.0)
        spot = jnp.where(row[:, :1] < tokens, jnp.sum(spots, axis=1, keepdims=True), FAR)
        s = jnp.dot(kbuf[shard, pl.ds(slots, FRESH), :], q_two[...], preferred_element_type=F32)
        s = jnp.where(spot <= meta[tile, 0:1, :], s, LOW)
        fresh[...] = s
        return s

    wide = min(1024, block)

    def top_of(s):
        return jnp.max(s.reshape(s.shape[0] // 8, 8, rows), axis=0)

    def phase(now, then, tile, shard_now, shard_then):
        if now is not None:
            s_now, f_now = now
            m_old = m_now[0:1, :]
            m_new = jnp.maximum(m_old, jnp.max(peak[...], axis=0, keepdims=True))
            fade = jnp.exp2(m_old - m_new)
            m_now[...] = jnp.broadcast_to(m_new, (8, rows))
            p = jnp.exp2((f_now[...] - m_new).astype(BF16))
            add = jnp.dot(vbuf[shard_now, :, pl.ds(slots, FRESH)], p, preferred_element_type=F32)
            acc[...] = acc[...] * fade + add
        if then is not None:
            s_then, f_then = then
            top = top_of(fresh_scores(tile, shard_then, f_then))
        for b in range(BLOCKS):
            weights = []
            for c in range(block // wide):
                start = b * block + c * wide
                if then is not None:
                    s = jnp.dot(kbuf[shard_then, pl.ds(start, wide), :], q_two[...], preferred_element_type=F32)
                    s_then[pl.ds(start, wide), :] = s
                    top = jnp.maximum(top, top_of(s))
                if now is not None:
                    weights.append(jnp.exp2((s_now[pl.ds(start, wide), :] - m_new).astype(BF16)))
            if now is not None:
                acc[...] += jnp.dot(
                    vbuf[shard_now, :, pl.ds(b * block, block)],
                    jnp.concatenate(weights, axis=0),
                    preferred_element_type=F32,
                )
        if then is not None:
            peak[...] = top

    def clear():
        acc[...] = jnp.zeros_like(acc)
        m_now[...] = jnp.full_like(m_now, LOW)

    def finish(k):
        total = acc[pl.ds(HEAD, 8), :]
        part_out[k] = (acc[pl.ds(0, HEAD), :] / total[0:1]).astype(BF16)
        part_log[k] = m_now[...] + jnp.log(total) * math.log2(math.e)

    a, b = (s_a, f_a), (s_b, f_b)
    clear()
    split_queries(0)
    phase(None, a, 0, None, 0)

    @pl.loop(0, peers)
    def _(t):
        shard = lax.rem(t, 2)
        tile = lax.rem(t + 1, peers)

        @pl.when(t + first_sends < peers)
        def _():
            q_copy(t + first_sends).start()

        @pl.when(t + 1 < peers)
        def _():
            q_copy(t + 1).wait_recv()
            meta_copy(t + 1).wait_recv()

        split_queries(tile)
        phase(a, b, tile, shard, shard)

        @pl.when(t == 0)
        def _():
            acc_own[...] = acc[...]
            m_own[...] = m_now[...]
            meta_partner().wait_recv()
            k_partner().wait_recv()

        @pl.when(t > 0)
        def _():
            finish(t)
            out_copy(t).start()
            log_copy(t).start()

        @pl.when(t + 1 < peers)
        def _():
            clear()
            phase(b, a, tile, shard, 1 - shard)

        @pl.when(t == 0)
        def _():
            v_partner().wait_recv()

        @pl.when(t + 1 == peers)
        def _():
            acc[...] = acc_own[...]
            m_now[...] = m_own[...]
            phase(b, None, None, shard, None)
            finish(0)

    for k in range(1, peers):
        out_copy(k).wait_recv()
        log_copy(k).wait_recv()
    logs = [part_log[0]] + [got_log[k] for k in range(1, peers)]
    top = functools.reduce(jnp.maximum, logs)
    shares = [jnp.exp2(log - top) for log in logs]
    whole = functools.reduce(jnp.add, shares)
    shares = [share / whole for share in shares]
    mixed = shares[0][0:1] * part_out[0].astype(F32)
    for k in range(1, peers):
        mixed += shares[k][0:1] * got_out[k].astype(F32)
    mixed = mixed.T.astype(BF16)
    for h in range(GROUP):
        attended[:, pl.ds(h * HEAD, HEAD)] = mixed[h * tokens : (h + 1) * tokens]

    w_load.wait()
    span = wbuf.shape[1] // columns

    def project(k):
        at = pl.ds(pl.multiple_of(to_column(k) * span, span), span)
        return jnp.dot(attended[...], wbuf[:, at], preferred_element_type=F32)

    @pl.loop(0, columns - 1)
    def _(s):
        k = columns - 1 - s
        proj_out[k] = project(k).astype(BF16)
        proj_copy(k).start()

    result = project(0)
    for k in range(columns - 1, 0, -1):
        proj_copy(k).wait_recv()
        result += proj_got[k].astype(F32)
    out_ref[...] = result.astype(BF16)

    for k in range(1, peers):
        q_copy(k).wait_send()
        meta_copy(k).wait_send()
        out_copy(k).wait_send()
        log_copy(k).wait_send()
    meta_partner().wait_send()
    k_partner().wait_send()
    v_partner().wait_send()
    for k in range(1, columns):
        proj_copy(k).wait_send()


def grid_of(count):
    return (2, count // 2) if count > 2 else (1, count)


def per_device(queries, cache_keys, stored_values, fresh_keys, fresh_values, positions, lengths, out_weight, sizes):
    ctx_size, tp_size = sizes
    grid_ctx, grid_tp = grid_of(ctx_size // 2), grid_of(tp_size)
    peers = ctx_size // 2
    tokens, width = queries.shape
    rows = tokens * GROUP
    slots = cache_keys.shape[0]
    span = out_weight.shape[1] // tp_size
    vmem = pl.BlockSpec(memory_space=pltpu.VMEM)
    anywhere = pl.BlockSpec(memory_space=pl.ANY)
    dma = pltpu.SemaphoreType.DMA
    return pl.pallas_call(
        functools.partial(kernel, grid_ctx, grid_tp),
        out_shape=jax.ShapeDtypeStruct((tokens, span), BF16),
        in_specs=[vmem, vmem, vmem, vmem, pl.BlockSpec(memory_space=pltpu.SMEM), anywhere, anywhere, anywhere],
        out_specs=vmem,
        scratch_shapes=[
            pltpu.VMEM((peers, HEAD, rows), BF16),
            pltpu.VMEM((2 * HEAD, rows), BF16),
            pltpu.VMEM((peers + 1, 8, rows), F32),
            pltpu.VMEM((2, slots + FRESH, 2 * HEAD), BF16),
            pltpu.VMEM((2, HEAD + ONES, slots + FRESH), BF16),
            pltpu.VMEM((slots, HEAD), BF16),
            pltpu.VMEM(out_weight.shape, BF16),
            pltpu.VMEM((slots, rows), F32),
            pltpu.VMEM((slots, rows), F32),
            pltpu.VMEM((FRESH, rows), F32),
            pltpu.VMEM((FRESH, rows), F32),
            pltpu.VMEM((8, rows), F32),
            pltpu.VMEM((8, rows), F32),
            pltpu.VMEM((HEAD + ONES, rows), F32),
            pltpu.VMEM((8, rows), F32),
            pltpu.VMEM((HEAD + ONES, rows), F32),
            pltpu.VMEM((peers, HEAD, rows), BF16),
            pltpu.VMEM((peers, 8, rows), F32),
            pltpu.VMEM((peers, HEAD, rows), BF16),
            pltpu.VMEM((peers, 8, rows), F32),
            pltpu.VMEM((tokens, width), BF16),
            pltpu.VMEM((tp_size, tokens, span), BF16),
            pltpu.VMEM((tp_size, tokens, span), BF16),
            dma((3,)),
            dma((peers,)),
            dma((peers,)),
            dma((peers + 1,)),
            dma((peers + 1,)),
            dma((2,)),
            dma((2,)),
            dma((peers,)),
            dma((peers,)),
            dma((peers,)),
            dma((peers,)),
            dma((tp_size,)),
            dma((tp_size,)),
        ],
        compiler_params=pltpu.CompilerParams(
            collective_id=0, has_side_effects=True, vmem_limit_bytes=60 * 1024 * 1024
        ),
        cost_estimate=pl.CostEstimate(
            flops=4 * peers * rows * 2 * (slots + FRESH) * HEAD + 2 * tokens * width * out_weight.shape[1],
            bytes_accessed=2 * (out_weight.size + 2 * cache_keys.size),
            transcendentals=peers * rows * 2 * (slots + FRESH),
        ),
    )(
        queries,
        fresh_keys,
        fresh_values,
        positions.reshape(1, tokens),
        lengths,
        cache_keys,
        stored_values,
        out_weight,
    )


def solution(mesh):
    placed = (
        P("ctx", "tp"),
        P("ctx", "tp"),
        P("ctx", "tp"),
        P("ctx", "tp"),
        P("ctx", "tp"),
        P("ctx"),
        P("ctx"),
        P("tp", None),
    )
    sizes = (mesh.shape["ctx"], mesh.shape["tp"])
    return jax.shard_map(
        functools.partial(per_device, sizes=sizes),
        mesh=mesh,
        in_specs=placed,
        out_specs=P("ctx", "tp"),
        check_vma=False,
    )
```

```python
import functools
import math

import jax
import jax.numpy as jnp
from jax import lax
from jax.experimental import pallas as pl
from jax.experimental.pallas import tpu as pltpu
from jax.sharding import PartitionSpec as P

HEAD = 128
GROUP = 8
FRESH = 128
BLOCKS = 4
LOW = -1e30
FAR = 1e9
ONES = 16
F32 = jnp.float32
BF16 = jnp.bfloat16
UNIT = math.log2(math.e) / math.sqrt(HEAD)
MESH = pl.DeviceIdType.MESH


def kernel(
    grid_ctx,
    grid_tp,
    q_ref,
    fk_ref,
    fv_ref,
    pos_ref,
    len_ref,
    k_hbm,
    v_hbm,
    w_hbm,
    out_ref,
    qbuf,
    q_two,
    meta,
    kbuf,
    vbuf,
    v_raw,
    wbuf,
    s_a,
    s_b,
    f_a,
    f_b,
    peak,
    m_now,
    acc,
    m_own,
    acc_own,
    part_out,
    part_log,
    got_out,
    got_log,
    attended,
    proj_out,
    proj_got,
    local_sem,
    q_send,
    q_recv,
    meta_send,
    meta_recv,
    kv_send,
    kv_recv,
    out_send,
    out_recv,
    log_send,
    log_recv,
    proj_send,
    proj_recv,
):
    nz, ny = grid_ctx
    tz, tx = grid_tp
    peers = nz * ny
    columns = tz * tx
    tokens = q_ref.shape[0]
    rows = tokens * GROUP
    slots = k_hbm.shape[0]
    block = slots // BLOCKS

    ctx = lax.axis_index("ctx")
    tp = lax.axis_index("tp")
    core = lax.rem(ctx, 2)
    chip = lax.div(ctx, 2)
    cz, cy = lax.div(chip, ny), lax.rem(chip, ny)
    pz, px = lax.div(tp, tx), lax.rem(tp, tx)
    partner = ctx + 1 - 2 * core

    def in_turn(k):
        return k + (1 - 2 * lax.rem(k, 2)) * lax.div(k + peers - 2, peers)

    def to_chip(turn):
        k = in_turn(turn)
        z = lax.rem(cz + nz - lax.div(k, ny), nz)
        y = lax.rem(cy + ny - lax.rem(k, ny), ny)
        return (z * ny + y) * 2 + core

    def from_chip(turn):
        k = in_turn(turn)
        z = lax.rem(cz + lax.div(k, ny), nz)
        y = lax.rem(cy + lax.rem(k, ny), ny)
        return (z * ny + y) * 2 + core

    def to_column(k):
        z = lax.rem(pz + lax.div(k, tx), tz)
        x = lax.rem(px + lax.rem(k, tx), tx)
        return z * tx + x

    def remote(src, dst, send, recv, where):
        return pltpu.make_async_remote_copy(
            src_ref=src, dst_ref=dst, send_sem=send, recv_sem=recv, device_id=where, device_id_type=MESH
        )

    def q_copy(k):
        return remote(qbuf.at[0], qbuf.at[k], q_send.at[k], q_recv.at[k], {"ctx": to_chip(k)})

    def meta_copy(k):
        return remote(meta.at[0], meta.at[k], meta_send.at[k], meta_recv.at[k], {"ctx": to_chip(k)})

    def meta_partner():
        return remote(meta.at[0], meta.at[peers], meta_send.at[peers], meta_recv.at[peers], {"ctx": partner})

    def k_partner():
        half = pl.ds(0, HEAD)
        return remote(kbuf.at[0, :, half], kbuf.at[1, :, half], kv_send.at[0], kv_recv.at[0], {"ctx": partner})

    def v_partner():
        return remote(vbuf.at[0], vbuf.at[1], kv_send.at[1], kv_recv.at[1], {"ctx": partner})

    def out_copy(k):
        return remote(part_out.at[k], got_out.at[k], out_send.at[k], out_recv.at[k], {"ctx": from_chip(k)})

    def log_copy(k):
        return remote(part_log.at[k], got_log.at[k], log_send.at[k], log_recv.at[k], {"ctx": from_chip(k)})

    def proj_copy(k):
        return remote(proj_out.at[k], proj_got.at[k], proj_send.at[k], proj_recv.at[k], {"tp": to_column(k)})

    k_load = pltpu.make_async_copy(k_hbm, kbuf.at[0, pl.ds(0, slots), pl.ds(0, HEAD)], local_sem.at[0])
    v_load = pltpu.make_async_copy(v_hbm, v_raw, local_sem.at[1])
    w_load = pltpu.make_async_copy(w_hbm, wbuf, local_sem.at[2])
    k_load.start()
    v_load.start()

    barrier = pltpu.get_barrier_semaphore()
    for k in range(1, peers):
        pl.semaphore_signal(barrier, inc=1, device_id={"ctx": to_chip(k)}, device_id_type=MESH)
    pl.semaphore_signal(barrier, inc=1, device_id={"ctx": partner}, device_id_type=MESH)
    for k in range(1, columns):
        pl.semaphore_signal(barrier, inc=1, device_id={"tp": to_column(k)}, device_id_type=MESH)

    stacked = jnp.concatenate([q_ref[:, h * HEAD : (h + 1) * HEAD].astype(F32) for h in range(GROUP)], axis=0)
    qbuf[0] = stacked.T.astype(BF16)
    meta[0] = jnp.broadcast_to(jnp.concatenate([pos_ref[...].astype(F32)] * GROUP, axis=1), (8, rows))
    spare = jnp.zeros((FRESH - tokens, HEAD), F32)
    fresh_keys = jnp.concatenate([fk_ref[...].astype(F32), spare], axis=0).astype(BF16)
    for half in range(2):
        kbuf[0, pl.ds(slots, FRESH), pl.ds(half * HEAD, HEAD)] = fresh_keys
    vbuf[0, pl.ds(0, HEAD), pl.ds(slots, FRESH)] = (
        jnp.concatenate([fv_ref[...].astype(F32), spare], axis=0).T.astype(BF16)
    )
    vbuf[0, pl.ds(HEAD, ONES), pl.ds(slots, FRESH)] = jnp.ones((ONES, FRESH), BF16)

    pl.semaphore_wait(barrier, peers - 1 + 1 + columns - 1)
    first_sends = min(3, peers)
    for k in range(1, first_sends):
        q_copy(k).start()
    for k in range(1, peers):
        meta_copy(k).start()
    meta_partner().start()

    filled = len_ref[0]
    k_load.wait()
    lead = kbuf[0, pl.ds(0, 16), pl.ds(0, HEAD)].astype(F32)[0:1]
    tidy = block // 2

    @pl.loop(0, slots // tidy)
    def _(c):
        at = pl.ds(pl.multiple_of(c * tidy, tidy), tidy)
        valid = lax.broadcasted_iota(jnp.int32, (tidy, HEAD), 0) + c * tidy < filled
        keys = jnp.where(valid, kbuf[0, at, pl.ds(0, HEAD)].astype(F32), lead).astype(BF16)
        kbuf[0, at, pl.ds(0, HEAD)] = keys
        kbuf[0, at, pl.ds(HEAD, HEAD)] = keys

    k_partner().start()
    v_load.wait()

    @pl.loop(0, slots // tidy)
    def _(c):
        at = pl.ds(pl.multiple_of(c * tidy, tidy), tidy)
        valid = lax.broadcasted_iota(jnp.int32, (HEAD, tidy), 1) + c * tidy < filled
        vbuf[0, pl.ds(0, HEAD), at] = jnp.where(valid, v_raw[at, :].astype(F32).T, 0.0).astype(BF16)
        vbuf[0, pl.ds(HEAD, ONES), at] = jnp.where(valid[:ONES], 1.0, 0.0).astype(BF16)

    v_partner().start()
    w_load.start()

    def split_queries(tile):
        scaled = qbuf[tile].astype(F32) * UNIT
        high = scaled.astype(BF16)
        q_two[pl.ds(0, HEAD), :] = high
        q_two[pl.ds(HEAD, HEAD), :] = (scaled - high.astype(F32)).astype(BF16)

    def fresh_scores(tile, shard, fresh):
        row = lax.broadcasted_iota(jnp.int32, (FRESH, FRESH), 0)
        lane = lax.broadcasted_iota(jnp.int32, (FRESH, FRESH), 1)
        spots = jnp.where(row == lane, meta[shard * peers, 0:1, pl.ds(0, FRESH)], 0.0)
        spot = jnp.where(row[:, :1] < tokens, jnp.sum(spots, axis=1, keepdims=True), FAR)
        s = jnp.dot(kbuf[shard, pl.ds(slots, FRESH), :], q_two[...], preferred_element_type=F32)
        s = jnp.where(spot <= meta[tile, 0:1, :], s, LOW)
        fresh[...] = s
        return s

    wide = min(1024, block)

    def top_of(s):
        return jnp.max(s.reshape(s.shape[0] // 8, 8, rows), axis=0)

    def phase(now, then, tile, shard_now, shard_then):
        if now is not None:
            s_now, f_now = now
            m_old = m_now[0:1, :]
            m_new = jnp.maximum(m_old, jnp.max(peak[...], axis=0, keepdims=True))
            fade = jnp.exp2(m_old - m_new)
            m_now[...] = jnp.broadcast_to(m_new, (8, rows))
            p = jnp.exp2((f_now[...] - m_new).astype(BF16))
            add = jnp.dot(vbuf[shard_now, :, pl.ds(slots, FRESH)], p, preferred_element_type=F32)
            acc[...] = acc[...] * fade + add
        if then is not None:
            s_then, f_then = then
            top = top_of(fresh_scores(tile, shard_then, f_then))
        for b in range(BLOCKS):
            weights = []
            for c in range(block // wide):
                start = b * block + c * wide
                if then is not None:
                    s = jnp.dot(kbuf[shard_then, pl.ds(start, wide), :], q_two[...], preferred_element_type=F32)
                    s_then[pl.ds(start, wide), :] = s
                    top = jnp.maximum(top, top_of(s))
                if now is not None:
                    weights.append(jnp.exp2((s_now[pl.ds(start, wide), :] - m_new).astype(BF16)))
            if now is not None:
                acc[...] += jnp.dot(
                    vbuf[shard_now, :, pl.ds(b * block, block)],
                    jnp.concatenate(weights, axis=0),
                    preferred_element_type=F32,
                )
        if then is not None:
            peak[...] = top

    def clear():
        acc[...] = jnp.zeros_like(acc)
        m_now[...] = jnp.full_like(m_now, LOW)

    def finish(k):
        total = acc[pl.ds(HEAD, 8), :]
        part_out[k] = (acc[pl.ds(0, HEAD), :] / total[0:1]).astype(BF16)
        part_log[k] = m_now[...] + jnp.log(total) * math.log2(math.e)

    a, b = (s_a, f_a), (s_b, f_b)
    clear()
    split_queries(0)
    phase(None, a, 0, None, 0)

    @pl.loop(0, peers)
    def _(t):
        shard = lax.rem(t, 2)
        tile = lax.rem(t + 1, peers)

        @pl.when(t + first_sends < peers)
        def _():
            q_copy(t + first_sends).start()

        @pl.when(t + 1 < peers)
        def _():
            q_copy(t + 1).wait_recv()
            meta_copy(t + 1).wait_recv()

        split_queries(tile)
        phase(a, b, tile, shard, shard)

        @pl.when(t == 0)
        def _():
            acc_own[...] = acc[...]
            m_own[...] = m_now[...]
            meta_partner().wait_recv()
            k_partner().wait_recv()

            @pl.loop(0, slots // tidy)
            def _(c):
                at = pl.ds(pl.multiple_of(c * tidy, tidy), tidy)
                kbuf[1, at, pl.ds(HEAD, HEAD)] = kbuf[1, at, pl.ds(0, HEAD)]

            kbuf[1, pl.ds(slots, FRESH), pl.ds(HEAD, HEAD)] = kbuf[1, pl.ds(slots, FRESH), pl.ds(0, HEAD)]

        @pl.when(t > 0)
        def _():
            finish(t)
            out_copy(t).start()
            log_copy(t).start()

        @pl.when(t + 1 < peers)
        def _():
            clear()
            phase(b, a, tile, shard, 1 - shard)

        @pl.when(t == 0)
        def _():
            v_partner().wait_recv()

        @pl.when(t + 1 == peers)
        def _():
            acc[...] = acc_own[...]
            m_now[...] = m_own[...]
            phase(b, None, None, shard, None)
            finish(0)

    for k in range(1, peers):
        out_copy(k).wait_recv()
        log_copy(k).wait_recv()
    logs = [part_log[0]] + [got_log[k] for k in range(1, peers)]
    top = functools.reduce(jnp.maximum, logs)
    shares = [jnp.exp2(log - top) for log in logs]
    whole = functools.reduce(jnp.add, shares)
    shares = [share / whole for share in shares]
    mixed = shares[0][0:1] * part_out[0].astype(F32)
    for k in range(1, peers):
        mixed += shares[k][0:1] * got_out[k].astype(F32)
    mixed = mixed.T.astype(BF16)
    for h in range(GROUP):
        attended[:, pl.ds(h * HEAD, HEAD)] = mixed[h * tokens : (h + 1) * tokens]

    w_load.wait()
    span = wbuf.shape[1] // columns

    def project(k):
        at = pl.ds(pl.multiple_of(to_column(k) * span, span), span)
        return jnp.dot(attended[...], wbuf[:, at], preferred_element_type=F32)

    @pl.loop(0, columns - 1)
    def _(s):
        k = columns - 1 - s
        proj_out[k] = project(k).astype(BF16)
        proj_copy(k).start()

    result = project(0)
    for k in range(columns - 1, 0, -1):
        proj_copy(k).wait_recv()
        result += proj_got[k].astype(F32)
    out_ref[...] = result.astype(BF16)

    for k in range(1, peers):
        q_copy(k).wait_send()
        meta_copy(k).wait_send()
        out_copy(k).wait_send()
        log_copy(k).wait_send()
    meta_partner().wait_send()
    k_partner().wait_send()
    v_partner().wait_send()
    for k in range(1, columns):
        proj_copy(k).wait_send()


def grid_of(count):
    return (2, count // 2) if count > 2 else (1, count)


def per_device(queries, cache_keys, stored_values, fresh_keys, fresh_values, positions, lengths, out_weight, sizes):
    ctx_size, tp_size = sizes
    grid_ctx, grid_tp = grid_of(ctx_size // 2), grid_of(tp_size)
    peers = ctx_size // 2
    tokens, width = queries.shape
    rows = tokens * GROUP
    slots = cache_keys.shape[0]
    span = out_weight.shape[1] // tp_size
    vmem = pl.BlockSpec(memory_space=pltpu.VMEM)
    anywhere = pl.BlockSpec(memory_space=pl.ANY)
    dma = pltpu.SemaphoreType.DMA
    return pl.pallas_call(
        functools.partial(kernel, grid_ctx, grid_tp),
        out_shape=jax.ShapeDtypeStruct((tokens, span), BF16),
        in_specs=[vmem, vmem, vmem, vmem, pl.BlockSpec(memory_space=pltpu.SMEM), anywhere, anywhere, anywhere],
        out_specs=vmem,
        scratch_shapes=[
            pltpu.VMEM((peers, HEAD, rows), BF16),
            pltpu.VMEM((2 * HEAD, rows), BF16),
            pltpu.VMEM((peers + 1, 8, rows), F32),
            pltpu.VMEM((2, slots + FRESH, 2 * HEAD), BF16),
            pltpu.VMEM((2, HEAD + ONES, slots + FRESH), BF16),
            pltpu.VMEM((slots, HEAD), BF16),
            pltpu.VMEM(out_weight.shape, BF16),
            pltpu.VMEM((slots, rows), F32),
            pltpu.VMEM((slots, rows), F32),
            pltpu.VMEM((FRESH, rows), F32),
            pltpu.VMEM((FRESH, rows), F32),
            pltpu.VMEM((8, rows), F32),
            pltpu.VMEM((8, rows), F32),
            pltpu.VMEM((HEAD + ONES, rows), F32),
            pltpu.VMEM((8, rows), F32),
            pltpu.VMEM((HEAD + ONES, rows), F32),
            pltpu.VMEM((peers, HEAD, rows), BF16),
            pltpu.VMEM((peers, 8, rows), F32),
            pltpu.VMEM((peers, HEAD, rows), BF16),
            pltpu.VMEM((peers, 8, rows), F32),
            pltpu.VMEM((tokens, width), BF16),
            pltpu.VMEM((tp_size, tokens, span), BF16),
            pltpu.VMEM((tp_size, tokens, span), BF16),
            dma((3,)),
            dma((peers,)),
            dma((peers,)),
            dma((peers + 1,)),
            dma((peers + 1,)),
            dma((2,)),
            dma((2,)),
            dma((peers,)),
            dma((peers,)),
            dma((peers,)),
            dma((peers,)),
            dma((tp_size,)),
            dma((tp_size,)),
        ],
        compiler_params=pltpu.CompilerParams(
            collective_id=0, has_side_effects=True, vmem_limit_bytes=60 * 1024 * 1024
        ),
        cost_estimate=pl.CostEstimate(
            flops=4 * peers * rows * 2 * (slots + FRESH) * HEAD + 2 * tokens * width * out_weight.shape[1],
            bytes_accessed=2 * (out_weight.size + 2 * cache_keys.size),
            transcendentals=peers * rows * 2 * (slots + FRESH),
        ),
    )(
        queries,
        fresh_keys,
        fresh_values,
        positions.reshape(1, tokens),
        lengths,
        cache_keys,
        stored_values,
        out_weight,
    )


def solution(mesh):
    placed = (
        P("ctx", "tp"),
        P("ctx", "tp"),
        P("ctx", "tp"),
        P("ctx", "tp"),
        P("ctx", "tp"),
        P("ctx"),
        P("ctx"),
        P("tp", None),
    )
    sizes = (mesh.shape["ctx"], mesh.shape["tp"])
    return jax.shard_map(
        functools.partial(per_device, sizes=sizes),
        mesh=mesh,
        in_specs=placed,
        out_specs=P("ctx", "tp"),
        check_vma=False,
    )
```

```python
import functools
import math

import jax
import jax.numpy as jnp
from jax import lax
from jax.experimental import pallas as pl
from jax.experimental.pallas import tpu as pltpu
from jax.sharding import PartitionSpec as P

HEAD = 128
GROUP = 8
FRESH = 128
BLOCKS = 4
LOW = -1e30
FAR = 1e9
ONES = 16
F32 = jnp.float32
BF16 = jnp.bfloat16
UNIT = math.log2(math.e) / math.sqrt(HEAD)
MESH = pl.DeviceIdType.MESH


def kernel(
    grid_ctx,
    grid_tp,
    q_ref,
    fk_ref,
    fv_ref,
    pos_ref,
    len_ref,
    k_hbm,
    v_hbm,
    w_hbm,
    out_ref,
    qbuf,
    q_two,
    meta,
    kbuf,
    vbuf,
    v_raw,
    wbuf,
    s_a,
    s_b,
    f_a,
    f_b,
    peak,
    m_now,
    acc,
    m_own,
    acc_own,
    part_out,
    part_log,
    got_out,
    got_log,
    attended,
    proj_out,
    proj_got,
    relay_out,
    relay_got,
    local_sem,
    q_send,
    q_recv,
    meta_send,
    meta_recv,
    kv_send,
    kv_recv,
    out_send,
    out_recv,
    log_send,
    log_recv,
    proj_send,
    proj_recv,
    relay_send,
    relay_recv,
):
    nz, ny = grid_ctx
    tz, tx = grid_tp
    peers = nz * ny
    columns = tz * tx
    tokens = q_ref.shape[0]
    rows = tokens * GROUP
    slots = k_hbm.shape[0]
    block = slots // BLOCKS

    ctx = lax.axis_index("ctx")
    tp = lax.axis_index("tp")
    core = lax.rem(ctx, 2)
    chip = lax.div(ctx, 2)
    cz, cy = lax.div(chip, ny), lax.rem(chip, ny)
    pz, px = lax.div(tp, tx), lax.rem(tp, tx)
    partner = ctx + 1 - 2 * core

    def in_turn(k):
        return k + (1 - 2 * lax.rem(k, 2)) * lax.div(k + peers - 2, peers)

    def to_chip(turn):
        k = in_turn(turn)
        z = lax.rem(cz + nz - lax.div(k, ny), nz)
        y = lax.rem(cy + ny - lax.rem(k, ny), ny)
        return (z * ny + y) * 2 + core

    def from_chip(turn):
        k = in_turn(turn)
        z = lax.rem(cz + lax.div(k, ny), nz)
        y = lax.rem(cy + lax.rem(k, ny), ny)
        return (z * ny + y) * 2 + core

    def to_column(k):
        z = lax.rem(pz + lax.div(k, tx), tz)
        x = lax.rem(px + lax.rem(k, tx), tx)
        return z * tx + x

    def remote(src, dst, send, recv, where):
        return pltpu.make_async_remote_copy(
            src_ref=src, dst_ref=dst, send_sem=send, recv_sem=recv, device_id=where, device_id_type=MESH
        )

    def q_copy(k):
        return remote(qbuf.at[0], qbuf.at[k], q_send.at[k], q_recv.at[k], {"ctx": to_chip(k)})

    def meta_copy(k):
        return remote(meta.at[0], meta.at[k], meta_send.at[k], meta_recv.at[k], {"ctx": to_chip(k)})

    def meta_partner():
        return remote(meta.at[0], meta.at[peers], meta_send.at[peers], meta_recv.at[peers], {"ctx": partner})

    def k_partner():
        half = pl.ds(0, HEAD)
        return remote(kbuf.at[0, :, half], kbuf.at[1, :, half], kv_send.at[0], kv_recv.at[0], {"ctx": partner})

    def v_partner():
        return remote(vbuf.at[0], vbuf.at[1], kv_send.at[1], kv_recv.at[1], {"ctx": partner})

    def out_copy(k):
        return remote(part_out.at[k], got_out.at[k], out_send.at[k], out_recv.at[k], {"ctx": from_chip(k)})

    def log_copy(k):
        return remote(part_log.at[k], got_log.at[k], log_send.at[k], log_recv.at[k], {"ctx": from_chip(k)})

    def proj_copy(k):
        return remote(proj_out.at[k], proj_got.at[k], proj_send.at[k], proj_recv.at[k], {"tp": to_column(k)})

    def relay_copy(dz, side):
        to = to_column(1 if side == 0 else tx - 1)
        sems = relay_send.at[2 * dz + side], relay_recv.at[2 * dz + side]
        return remote(relay_out.at[dz, side], relay_got.at[dz, side], *sems, {"tp": to})

    k_load = pltpu.make_async_copy(k_hbm, kbuf.at[0, pl.ds(0, slots), pl.ds(0, HEAD)], local_sem.at[0])
    v_load = pltpu.make_async_copy(v_hbm, v_raw, local_sem.at[1])
    w_load = pltpu.make_async_copy(w_hbm, wbuf, local_sem.at[2])
    k_load.start()
    v_load.start()

    barrier = pltpu.get_barrier_semaphore()
    for k in range(1, peers):
        pl.semaphore_signal(barrier, inc=1, device_id={"ctx": to_chip(k)}, device_id_type=MESH)
    pl.semaphore_signal(barrier, inc=1, device_id={"ctx": partner}, device_id_type=MESH)
    for k in range(1, columns):
        pl.semaphore_signal(barrier, inc=1, device_id={"tp": to_column(k)}, device_id_type=MESH)

    stacked = jnp.concatenate([q_ref[:, h * HEAD : (h + 1) * HEAD].astype(F32) for h in range(GROUP)], axis=0)
    qbuf[0] = stacked.T.astype(BF16)
    meta[0] = jnp.broadcast_to(jnp.concatenate([pos_ref[...].astype(F32)] * GROUP, axis=1), (8, rows))
    spare = jnp.zeros((FRESH - tokens, HEAD), F32)
    fresh_keys = jnp.concatenate([fk_ref[...].astype(F32), spare], axis=0).astype(BF16)
    for half in range(2):
        kbuf[0, pl.ds(slots, FRESH), pl.ds(half * HEAD, HEAD)] = fresh_keys
    vbuf[0, pl.ds(0, HEAD), pl.ds(slots, FRESH)] = (
        jnp.concatenate([fv_ref[...].astype(F32), spare], axis=0).T.astype(BF16)
    )
    vbuf[0, pl.ds(HEAD, ONES), pl.ds(slots, FRESH)] = jnp.ones((ONES, FRESH), BF16)

    pl.semaphore_wait(barrier, peers - 1 + 1 + columns - 1)
    first_sends = min(3, peers)
    for k in range(1, first_sends):
        q_copy(k).start()
    for k in range(1, peers):
        meta_copy(k).start()
    meta_partner().start()

    filled = len_ref[0]
    k_load.wait()
    lead = kbuf[0, pl.ds(0, 16), pl.ds(0, HEAD)].astype(F32)[0:1]
    tidy = block // 2

    @pl.loop(0, slots // tidy)
    def _(c):
        at = pl.ds(pl.multiple_of(c * tidy, tidy), tidy)
        valid = lax.broadcasted_iota(jnp.int32, (tidy, HEAD), 0) + c * tidy < filled
        keys = jnp.where(valid, kbuf[0, at, pl.ds(0, HEAD)].astype(F32), lead).astype(BF16)
        kbuf[0, at, pl.ds(0, HEAD)] = keys
        kbuf[0, at, pl.ds(HEAD, HEAD)] = keys

    k_partner().start()
    v_load.wait()

    @pl.loop(0, slots // tidy)
    def _(c):
        at = pl.ds(pl.multiple_of(c * tidy, tidy), tidy)
        valid = lax.broadcasted_iota(jnp.int32, (HEAD, tidy), 1) + c * tidy < filled
        vbuf[0, pl.ds(0, HEAD), at] = jnp.where(valid, v_raw[at, :].astype(F32).T, 0.0).astype(BF16)
        vbuf[0, pl.ds(HEAD, ONES), at] = jnp.where(valid[:ONES], 1.0, 0.0).astype(BF16)

    v_partner().start()
    w_load.start()

    def split_queries(tile):
        scaled = qbuf[tile].astype(F32) * UNIT
        high = scaled.astype(BF16)
        q_two[pl.ds(0, HEAD), :] = high
        q_two[pl.ds(HEAD, HEAD), :] = (scaled - high.astype(F32)).astype(BF16)

    def fresh_scores(tile, shard, fresh):
        row = lax.broadcasted_iota(jnp.int32, (FRESH, FRESH), 0)
        lane = lax.broadcasted_iota(jnp.int32, (FRESH, FRESH), 1)
        spots = jnp.where(row == lane, meta[shard * peers, 0:1, pl.ds(0, FRESH)], 0.0)
        spot = jnp.where(row[:, :1] < tokens, jnp.sum(spots, axis=1, keepdims=True), FAR)
        s = jnp.dot(kbuf[shard, pl.ds(slots, FRESH), :], q_two[...], preferred_element_type=F32)
        s = jnp.where(spot <= meta[tile, 0:1, :], s, LOW)
        fresh[...] = s
        return s

    wide = min(1024, block)

    def top_of(s):
        return jnp.max(s.reshape(s.shape[0] // 8, 8, rows), axis=0)

    def phase(now, then, tile, shard_now, shard_then):
        if now is not None:
            s_now, f_now = now
            m_old = m_now[0:1, :]
            m_new = jnp.maximum(m_old, jnp.max(peak[...], axis=0, keepdims=True))
            fade = jnp.exp2(m_old - m_new)
            m_now[...] = jnp.broadcast_to(m_new, (8, rows))
            p = jnp.exp2((f_now[...] - m_new).astype(BF16))
            add = jnp.dot(vbuf[shard_now, :, pl.ds(slots, FRESH)], p, preferred_element_type=F32)
            acc[...] = acc[...] * fade + add
        if then is not None:
            s_then, f_then = then
            top = top_of(fresh_scores(tile, shard_then, f_then))
        for b in range(BLOCKS):
            weights = []
            for c in range(block // wide):
                start = b * block + c * wide
                if then is not None:
                    s = jnp.dot(kbuf[shard_then, pl.ds(start, wide), :], q_two[...], preferred_element_type=F32)
                    s_then[pl.ds(start, wide), :] = s
                    top = jnp.maximum(top, top_of(s))
                if now is not None:
                    weights.append(jnp.exp2((s_now[pl.ds(start, wide), :] - m_new).astype(BF16)))
            if now is not None:
                acc[...] += jnp.dot(
                    vbuf[shard_now, :, pl.ds(b * block, block)],
                    jnp.concatenate(weights, axis=0),
                    preferred_element_type=F32,
                )
        if then is not None:
            peak[...] = top

    def clear():
        acc[...] = jnp.zeros_like(acc)
        m_now[...] = jnp.full_like(m_now, LOW)

    def finish(k):
        total = acc[pl.ds(HEAD, 8), :]
        part_out[k] = (acc[pl.ds(0, HEAD), :] / total[0:1]).astype(BF16)
        part_log[k] = m_now[...] + jnp.log(total) * math.log2(math.e)

    a, b = (s_a, f_a), (s_b, f_b)
    clear()
    split_queries(0)
    phase(None, a, 0, None, 0)

    @pl.loop(0, peers)
    def _(t):
        shard = lax.rem(t, 2)
        tile = lax.rem(t + 1, peers)

        @pl.when(t + first_sends < peers)
        def _():
            q_copy(t + first_sends).start()

        @pl.when(t + 1 < peers)
        def _():
            q_copy(t + 1).wait_recv()
            meta_copy(t + 1).wait_recv()

        split_queries(tile)
        phase(a, b, tile, shard, shard)

        @pl.when(t == 0)
        def _():
            acc_own[...] = acc[...]
            m_own[...] = m_now[...]
            meta_partner().wait_recv()
            k_partner().wait_recv()

            @pl.loop(0, slots // tidy)
            def _(c):
                at = pl.ds(pl.multiple_of(c * tidy, tidy), tidy)
                kbuf[1, at, pl.ds(HEAD, HEAD)] = kbuf[1, at, pl.ds(0, HEAD)]

            kbuf[1, pl.ds(slots, FRESH), pl.ds(HEAD, HEAD)] = kbuf[1, pl.ds(slots, FRESH), pl.ds(0, HEAD)]

        @pl.when(t > 0)
        def _():
            finish(t)
            out_copy(t).start()
            log_copy(t).start()

        @pl.when(t + 1 < peers)
        def _():
            clear()
            phase(b, a, tile, shard, 1 - shard)

        @pl.when(t == 0)
        def _():
            v_partner().wait_recv()

        @pl.when(t + 1 == peers)
        def _():
            acc[...] = acc_own[...]
            m_now[...] = m_own[...]
            phase(b, None, None, shard, None)
            finish(0)

    for k in range(1, peers):
        out_copy(k).wait_recv()
        log_copy(k).wait_recv()
    logs = [part_log[0]] + [got_log[k] for k in range(1, peers)]
    top = functools.reduce(jnp.maximum, logs)
    shares = [jnp.exp2(log - top) for log in logs]
    whole = functools.reduce(jnp.add, shares)
    shares = [share / whole for share in shares]
    mixed = shares[0][0:1] * part_out[0].astype(F32)
    for k in range(1, peers):
        mixed += shares[k][0:1] * got_out[k].astype(F32)
    mixed = mixed.T.astype(BF16)
    for h in range(GROUP):
        attended[:, pl.ds(h * HEAD, HEAD)] = mixed[h * tokens : (h + 1) * tokens]

    w_load.wait()
    span = wbuf.shape[1] // columns

    def project(k):
        at = pl.ds(pl.multiple_of(to_column(k) * span, span), span)
        return jnp.dot(attended[...], wbuf[:, at], preferred_element_type=F32)

    def send_projected(k, terms):
        proj_out[k] = terms.astype(BF16)
        proj_copy(k).start()

    relayed = tx == 4
    side_span = span // 2
    if relayed:
        direct = [dz * tx for dz in range(tz - 1, 0, -1)]
        joined = [(dz, side) for dz in range(tz - 1, -1, -1) for side in range(2)]
        for dz in range(tz - 1, -1, -1):
            terms = project(dz * tx + 2).astype(BF16)
            for side in range(2):
                relay_out[dz, side] = terms[:, side * side_span : (side + 1) * side_span]
                relay_copy(dz, side).start()
    else:
        direct = list(range(columns - 1, 0, -1))
        joined = []
    for k in direct:
        send_projected(k, project(k))
    for dz, side in joined:
        k = dz * tx + (1 if side == 0 else tx - 1)
        terms = project(k)
        relay_copy(dz, side).wait_recv()
        left, right = terms[:, :side_span], terms[:, side_span:]
        more = relay_got[dz, side].astype(F32)
        halves = [left + more, right] if side == 0 else [left, right + more]
        send_projected(k, jnp.concatenate(halves, axis=1))
    sent = direct + [dz * tx + (1 if side == 0 else tx - 1) for dz, side in joined]

    result = project(0)
    for k in sent:
        proj_copy(k).wait_recv()
        result += proj_got[k].astype(F32)
    out_ref[...] = result.astype(BF16)

    for k in range(1, peers):
        q_copy(k).wait_send()
        meta_copy(k).wait_send()
        out_copy(k).wait_send()
        log_copy(k).wait_send()
    meta_partner().wait_send()
    k_partner().wait_send()
    v_partner().wait_send()
    for k in sent:
        proj_copy(k).wait_send()
    for dz, side in joined:
        relay_copy(dz, side).wait_send()


def grid_of(count):
    return (2, count // 2) if count > 4 else (1, count)


def per_device(queries, cache_keys, stored_values, fresh_keys, fresh_values, positions, lengths, out_weight, sizes):
    ctx_size, tp_size = sizes
    grid_ctx, grid_tp = grid_of(ctx_size // 2), grid_of(tp_size)
    peers = ctx_size // 2
    tokens, width = queries.shape
    rows = tokens * GROUP
    slots = cache_keys.shape[0]
    span = out_weight.shape[1] // tp_size
    vmem = pl.BlockSpec(memory_space=pltpu.VMEM)
    anywhere = pl.BlockSpec(memory_space=pl.ANY)
    dma = pltpu.SemaphoreType.DMA
    return pl.pallas_call(
        functools.partial(kernel, grid_ctx, grid_tp),
        out_shape=jax.ShapeDtypeStruct((tokens, span), BF16),
        in_specs=[vmem, vmem, vmem, vmem, pl.BlockSpec(memory_space=pltpu.SMEM), anywhere, anywhere, anywhere],
        out_specs=vmem,
        scratch_shapes=[
            pltpu.VMEM((peers, HEAD, rows), BF16),
            pltpu.VMEM((2 * HEAD, rows), BF16),
            pltpu.VMEM((peers + 1, 8, rows), F32),
            pltpu.VMEM((2, slots + FRESH, 2 * HEAD), BF16),
            pltpu.VMEM((2, HEAD + ONES, slots + FRESH), BF16),
            pltpu.VMEM((slots, HEAD), BF16),
            pltpu.VMEM(out_weight.shape, BF16),
            pltpu.VMEM((slots, rows), F32),
            pltpu.VMEM((slots, rows), F32),
            pltpu.VMEM((FRESH, rows), F32),
            pltpu.VMEM((FRESH, rows), F32),
            pltpu.VMEM((8, rows), F32),
            pltpu.VMEM((8, rows), F32),
            pltpu.VMEM((HEAD + ONES, rows), F32),
            pltpu.VMEM((8, rows), F32),
            pltpu.VMEM((HEAD + ONES, rows), F32),
            pltpu.VMEM((peers, HEAD, rows), BF16),
            pltpu.VMEM((peers, 8, rows), F32),
            pltpu.VMEM((peers, HEAD, rows), BF16),
            pltpu.VMEM((peers, 8, rows), F32),
            pltpu.VMEM((tokens, width), BF16),
            pltpu.VMEM((tp_size, tokens, span), BF16),
            pltpu.VMEM((tp_size, tokens, span), BF16),
            pltpu.VMEM((grid_tp[0], 2, tokens, span // 2), BF16),
            pltpu.VMEM((grid_tp[0], 2, tokens, span // 2), BF16),
            dma((3,)),
            dma((peers,)),
            dma((peers,)),
            dma((peers + 1,)),
            dma((peers + 1,)),
            dma((2,)),
            dma((2,)),
            dma((peers,)),
            dma((peers,)),
            dma((peers,)),
            dma((peers,)),
            dma((tp_size,)),
            dma((tp_size,)),
            dma((2 * grid_tp[0],)),
            dma((2 * grid_tp[0],)),
        ],
        compiler_params=pltpu.CompilerParams(
            collective_id=0, has_side_effects=True, vmem_limit_bytes=60 * 1024 * 1024
        ),
        cost_estimate=pl.CostEstimate(
            flops=4 * peers * rows * 2 * (slots + FRESH) * HEAD + 2 * tokens * width * out_weight.shape[1],
            bytes_accessed=2 * (out_weight.size + 2 * cache_keys.size),
            transcendentals=peers * rows * 2 * (slots + FRESH),
        ),
    )(
        queries,
        fresh_keys,
        fresh_values,
        positions.reshape(1, tokens),
        lengths,
        cache_keys,
        stored_values,
        out_weight,
    )


def solution(mesh):
    placed = (
        P("ctx", "tp"),
        P("ctx", "tp"),
        P("ctx", "tp"),
        P("ctx", "tp"),
        P("ctx", "tp"),
        P("ctx"),
        P("ctx"),
        P("tp", None),
    )
    sizes = (mesh.shape["ctx"], mesh.shape["tp"])
    return jax.shard_map(
        functools.partial(per_device, sizes=sizes),
        mesh=mesh,
        in_specs=placed,
        out_specs=P("ctx", "tp"),
        check_vma=False,
    )
```

```python
import functools
import math

import jax
import jax.numpy as jnp
from jax import lax
from jax.experimental import pallas as pl
from jax.experimental.pallas import tpu as pltpu
from jax.sharding import PartitionSpec as P

HEAD = 128
GROUP = 8
FRESH = 128
BLOCKS = 4
LOW = -1e30
FAR = 1e9
ONES = 16
F32 = jnp.float32
BF16 = jnp.bfloat16
UNIT = math.log2(math.e) / math.sqrt(HEAD)
MESH = pl.DeviceIdType.MESH


def kernel(
    grid_ctx,
    grid_tp,
    q_ref,
    fk_ref,
    fv_ref,
    pos_ref,
    len_ref,
    k_hbm,
    v_hbm,
    w_hbm,
    out_ref,
    qbuf,
    q_two,
    meta,
    kbuf,
    vbuf,
    v_raw,
    wbuf,
    s_a,
    s_b,
    f_a,
    f_b,
    peak,
    m_now,
    acc,
    m_own,
    acc_own,
    part_out,
    part_log,
    got_out,
    got_log,
    attended,
    proj_out,
    proj_got,
    relay_out,
    relay_got,
    local_sem,
    q_send,
    q_recv,
    meta_send,
    meta_recv,
    kv_send,
    kv_recv,
    out_send,
    out_recv,
    log_send,
    log_recv,
    proj_send,
    proj_recv,
    relay_send,
    relay_recv,
):
    nz, ny = grid_ctx
    tz, tx = grid_tp
    peers = nz * ny
    columns = tz * tx
    tokens = q_ref.shape[0]
    rows = tokens * GROUP
    slots = k_hbm.shape[0]
    block = slots // BLOCKS

    ctx = lax.axis_index("ctx")
    tp = lax.axis_index("tp")
    core = lax.rem(ctx, 2)
    chip = lax.div(ctx, 2)
    cz, cy = lax.div(chip, ny), lax.rem(chip, ny)
    pz, px = lax.div(tp, tx), lax.rem(tp, tx)
    partner = ctx + 1 - 2 * core

    def in_turn(k):
        return k + (1 - 2 * lax.rem(k, 2)) * lax.div(k + peers - 2, peers)

    def to_chip(turn):
        k = in_turn(turn)
        z = lax.rem(cz + nz - lax.div(k, ny), nz)
        y = lax.rem(cy + ny - lax.rem(k, ny), ny)
        return (z * ny + y) * 2 + core

    def from_chip(turn):
        k = in_turn(turn)
        z = lax.rem(cz + lax.div(k, ny), nz)
        y = lax.rem(cy + lax.rem(k, ny), ny)
        return (z * ny + y) * 2 + core

    def to_column(k):
        z = lax.rem(pz + lax.div(k, tx), tz)
        x = lax.rem(px + lax.rem(k, tx), tx)
        return z * tx + x

    def remote(src, dst, send, recv, where):
        return pltpu.make_async_remote_copy(
            src_ref=src, dst_ref=dst, send_sem=send, recv_sem=recv, device_id=where, device_id_type=MESH
        )

    def q_copy(k):
        return remote(qbuf.at[0], qbuf.at[k], q_send.at[k], q_recv.at[k], {"ctx": to_chip(k)})

    def meta_copy(k):
        return remote(meta.at[0], meta.at[k], meta_send.at[k], meta_recv.at[k], {"ctx": to_chip(k)})

    def meta_partner():
        return remote(meta.at[0], meta.at[peers], meta_send.at[peers], meta_recv.at[peers], {"ctx": partner})

    def k_partner():
        half = pl.ds(0, HEAD)
        return remote(kbuf.at[0, :, half], kbuf.at[1, :, half], kv_send.at[0], kv_recv.at[0], {"ctx": partner})

    def v_partner():
        return remote(vbuf.at[0], vbuf.at[1], kv_send.at[1], kv_recv.at[1], {"ctx": partner})

    def out_copy(k):
        return remote(part_out.at[k], got_out.at[k], out_send.at[k], out_recv.at[k], {"ctx": from_chip(k)})

    def log_copy(k):
        return remote(part_log.at[k], got_log.at[k], log_send.at[k], log_recv.at[k], {"ctx": from_chip(k)})

    def proj_copy(k):
        return remote(proj_out.at[k], proj_got.at[k], proj_send.at[k], proj_recv.at[k], {"tp": to_column(k)})

    def relay_copy(dz, side):
        to = to_column(1 if side == 0 else tx - 1)
        sems = relay_send.at[2 * dz + side], relay_recv.at[2 * dz + side]
        return remote(relay_out.at[dz, side], relay_got.at[dz, side], *sems, {"tp": to})

    k_load = pltpu.make_async_copy(k_hbm, kbuf.at[0, pl.ds(0, slots), pl.ds(0, HEAD)], local_sem.at[0])
    v_load = pltpu.make_async_copy(v_hbm, v_raw, local_sem.at[1])
    w_load = pltpu.make_async_copy(w_hbm, wbuf, local_sem.at[2])
    k_load.start()
    v_load.start()

    barrier = pltpu.get_barrier_semaphore()
    for k in range(1, peers):
        pl.semaphore_signal(barrier, inc=1, device_id={"ctx": to_chip(k)}, device_id_type=MESH)
    pl.semaphore_signal(barrier, inc=1, device_id={"ctx": partner}, device_id_type=MESH)
    for k in range(1, columns):
        pl.semaphore_signal(barrier, inc=1, device_id={"tp": to_column(k)}, device_id_type=MESH)

    stacked = jnp.concatenate([q_ref[:, h * HEAD : (h + 1) * HEAD].astype(F32) for h in range(GROUP)], axis=0)
    qbuf[0] = stacked.T.astype(BF16)
    meta[0] = jnp.broadcast_to(jnp.concatenate([pos_ref[...].astype(F32)] * GROUP, axis=1), (8, rows))
    spare = jnp.zeros((FRESH - tokens, HEAD), F32)
    fresh_keys = jnp.concatenate([fk_ref[...].astype(F32), spare], axis=0).astype(BF16)
    for half in range(2):
        kbuf[0, pl.ds(slots, FRESH), pl.ds(half * HEAD, HEAD)] = fresh_keys
    vbuf[0, pl.ds(0, HEAD), pl.ds(slots, FRESH)] = (
        jnp.concatenate([fv_ref[...].astype(F32), spare], axis=0).T.astype(BF16)
    )
    vbuf[0, pl.ds(HEAD, ONES), pl.ds(slots, FRESH)] = jnp.ones((ONES, FRESH), BF16)

    pl.semaphore_wait(barrier, peers - 1 + 1 + columns - 1)
    first_sends = min(3, peers)
    for k in range(1, first_sends):
        q_copy(k).start()
    for k in range(1, peers):
        meta_copy(k).start()
    meta_partner().start()

    filled = len_ref[0]
    k_load.wait()
    lead = kbuf[0, pl.ds(0, 16), pl.ds(0, HEAD)].astype(F32)[0:1]
    tidy = block // 2

    @pl.loop(0, slots // tidy)
    def _(c):
        at = pl.ds(pl.multiple_of(c * tidy, tidy), tidy)
        valid = lax.broadcasted_iota(jnp.int32, (tidy, HEAD), 0) + c * tidy < filled
        keys = jnp.where(valid, kbuf[0, at, pl.ds(0, HEAD)].astype(F32), lead).astype(BF16)
        kbuf[0, at, pl.ds(0, HEAD)] = keys
        kbuf[0, at, pl.ds(HEAD, HEAD)] = keys

    k_partner().start()
    v_load.wait()

    def tidy_values(b):
        at = pl.ds(b * block, block)
        valid = lax.broadcasted_iota(jnp.int32, (HEAD, block), 1) + b * block < filled
        vbuf[0, pl.ds(0, HEAD), at] = jnp.where(valid, v_raw[at, :].astype(F32).T, 0.0).astype(BF16)
        vbuf[0, pl.ds(HEAD, ONES), at] = jnp.where(valid[:ONES], 1.0, 0.0).astype(BF16)

    def split_queries(tile):
        scaled = qbuf[tile].astype(F32) * UNIT
        high = scaled.astype(BF16)
        q_two[pl.ds(0, HEAD), :] = high
        q_two[pl.ds(HEAD, HEAD), :] = (scaled - high.astype(F32)).astype(BF16)

    def fresh_scores(tile, shard, fresh):
        row = lax.broadcasted_iota(jnp.int32, (FRESH, FRESH), 0)
        lane = lax.broadcasted_iota(jnp.int32, (FRESH, FRESH), 1)
        spots = jnp.where(row == lane, meta[shard * peers, 0:1, pl.ds(0, FRESH)], 0.0)
        spot = jnp.where(row[:, :1] < tokens, jnp.sum(spots, axis=1, keepdims=True), FAR)
        s = jnp.dot(kbuf[shard, pl.ds(slots, FRESH), :], q_two[...], preferred_element_type=F32)
        s = jnp.where(spot <= meta[tile, 0:1, :], s, LOW)
        fresh[...] = s
        return s

    wide = min(1024, block)

    def top_of(s):
        return jnp.max(s.reshape(s.shape[0] // 8, 8, rows), axis=0)

    def phase(now, then, tile, shard_now, shard_then, beside=None):
        if now is not None:
            s_now, f_now = now
            m_old = m_now[0:1, :]
            m_new = jnp.maximum(m_old, jnp.max(peak[...], axis=0, keepdims=True))
            fade = jnp.exp2(m_old - m_new)
            m_now[...] = jnp.broadcast_to(m_new, (8, rows))
            p = jnp.exp2((f_now[...] - m_new).astype(BF16))
            add = jnp.dot(vbuf[shard_now, :, pl.ds(slots, FRESH)], p, preferred_element_type=F32)
            acc[...] = acc[...] * fade + add
        if then is not None:
            s_then, f_then = then
            top = top_of(fresh_scores(tile, shard_then, f_then))
        for b in range(BLOCKS):
            if beside is not None:
                beside(b)
            weights = []
            for c in range(block // wide):
                start = b * block + c * wide
                if then is not None:
                    s = jnp.dot(kbuf[shard_then, pl.ds(start, wide), :], q_two[...], preferred_element_type=F32)
                    s_then[pl.ds(start, wide), :] = s
                    top = jnp.maximum(top, top_of(s))
                if now is not None:
                    weights.append(jnp.exp2((s_now[pl.ds(start, wide), :] - m_new).astype(BF16)))
            if now is not None:
                acc[...] += jnp.dot(
                    vbuf[shard_now, :, pl.ds(b * block, block)],
                    jnp.concatenate(weights, axis=0),
                    preferred_element_type=F32,
                )
        if then is not None:
            peak[...] = top

    def clear():
        acc[...] = jnp.zeros_like(acc)
        m_now[...] = jnp.full_like(m_now, LOW)

    def finish(k):
        total = acc[pl.ds(HEAD, 8), :]
        part_out[k] = (acc[pl.ds(0, HEAD), :] / total[0:1]).astype(BF16)
        part_log[k] = m_now[...] + jnp.log(total) * math.log2(math.e)

    a, b = (s_a, f_a), (s_b, f_b)
    clear()
    split_queries(0)
    phase(None, a, 0, None, 0, tidy_values)
    v_partner().start()
    w_load.start()

    @pl.loop(0, peers)
    def _(t):
        shard = lax.rem(t, 2)
        tile = lax.rem(t + 1, peers)

        @pl.when(t + first_sends < peers)
        def _():
            q_copy(t + first_sends).start()

        @pl.when(t + 1 < peers)
        def _():
            q_copy(t + 1).wait_recv()
            meta_copy(t + 1).wait_recv()

        split_queries(tile)
        phase(a, b, tile, shard, shard)

        @pl.when(t == 0)
        def _():
            acc_own[...] = acc[...]
            m_own[...] = m_now[...]
            meta_partner().wait_recv()
            k_partner().wait_recv()

            @pl.loop(0, slots // tidy)
            def _(c):
                at = pl.ds(pl.multiple_of(c * tidy, tidy), tidy)
                kbuf[1, at, pl.ds(HEAD, HEAD)] = kbuf[1, at, pl.ds(0, HEAD)]

            kbuf[1, pl.ds(slots, FRESH), pl.ds(HEAD, HEAD)] = kbuf[1, pl.ds(slots, FRESH), pl.ds(0, HEAD)]

        @pl.when(t > 0)
        def _():
            finish(t)
            out_copy(t).start()
            log_copy(t).start()

        @pl.when(t + 1 < peers)
        def _():
            clear()
            phase(b, a, tile, shard, 1 - shard)

        @pl.when(t == 0)
        def _():
            v_partner().wait_recv()

        @pl.when(t + 1 == peers)
        def _():
            acc[...] = acc_own[...]
            m_now[...] = m_own[...]
            phase(b, None, None, shard, None)
            finish(0)

    for k in range(1, peers):
        out_copy(k).wait_recv()
        log_copy(k).wait_recv()
    logs = [part_log[0]] + [got_log[k] for k in range(1, peers)]
    top = functools.reduce(jnp.maximum, logs)
    shares = [jnp.exp2(log - top) for log in logs]
    whole = functools.reduce(jnp.add, shares)
    shares = [share / whole for share in shares]
    mixed = shares[0][0:1] * part_out[0].astype(F32)
    for k in range(1, peers):
        mixed += shares[k][0:1] * got_out[k].astype(F32)
    mixed = mixed.T.astype(BF16)
    for h in range(GROUP):
        attended[:, pl.ds(h * HEAD, HEAD)] = mixed[h * tokens : (h + 1) * tokens]

    w_load.wait()
    span = wbuf.shape[1] // columns

    def project(k):
        at = pl.ds(pl.multiple_of(to_column(k) * span, span), span)
        return jnp.dot(attended[...], wbuf[:, at], preferred_element_type=F32)

    def send_projected(k, terms):
        proj_out[k] = terms.astype(BF16)
        proj_copy(k).start()

    relayed = tx == 4
    side_span = span // 2
    if relayed:
        direct = [dz * tx for dz in range(tz - 1, 0, -1)]
        joined = [(dz, side) for dz in range(tz - 1, -1, -1) for side in range(2)]
        for dz in range(tz - 1, -1, -1):
            terms = project(dz * tx + 2).astype(BF16)
            for side in range(2):
                relay_out[dz, side] = terms[:, side * side_span : (side + 1) * side_span]
                relay_copy(dz, side).start()
    else:
        direct = list(range(columns - 1, 0, -1))
        joined = []
    for k in direct:
        send_projected(k, project(k))
    for dz, side in joined:
        k = dz * tx + (1 if side == 0 else tx - 1)
        terms = project(k)
        relay_copy(dz, side).wait_recv()
        left, right = terms[:, :side_span], terms[:, side_span:]
        more = relay_got[dz, side].astype(F32)
        halves = [left + more, right] if side == 0 else [left, right + more]
        send_projected(k, jnp.concatenate(halves, axis=1))
    sent = direct + [dz * tx + (1 if side == 0 else tx - 1) for dz, side in joined]

    result = project(0)
    for k in sent:
        proj_copy(k).wait_recv()
        result += proj_got[k].astype(F32)
    out_ref[...] = result.astype(BF16)

    for k in range(1, peers):
        q_copy(k).wait_send()
        meta_copy(k).wait_send()
        out_copy(k).wait_send()
        log_copy(k).wait_send()
    meta_partner().wait_send()
    k_partner().wait_send()
    v_partner().wait_send()
    for k in sent:
        proj_copy(k).wait_send()
    for dz, side in joined:
        relay_copy(dz, side).wait_send()


def grid_of(count):
    return (2, count // 2) if count > 4 else (1, count)


def per_device(queries, cache_keys, stored_values, fresh_keys, fresh_values, positions, lengths, out_weight, sizes):
    ctx_size, tp_size = sizes
    grid_ctx, grid_tp = grid_of(ctx_size // 2), grid_of(tp_size)
    peers = ctx_size // 2
    tokens, width = queries.shape
    rows = tokens * GROUP
    slots = cache_keys.shape[0]
    span = out_weight.shape[1] // tp_size
    vmem = pl.BlockSpec(memory_space=pltpu.VMEM)
    anywhere = pl.BlockSpec(memory_space=pl.ANY)
    dma = pltpu.SemaphoreType.DMA
    return pl.pallas_call(
        functools.partial(kernel, grid_ctx, grid_tp),
        out_shape=jax.ShapeDtypeStruct((tokens, span), BF16),
        in_specs=[vmem, vmem, vmem, vmem, pl.BlockSpec(memory_space=pltpu.SMEM), anywhere, anywhere, anywhere],
        out_specs=vmem,
        scratch_shapes=[
            pltpu.VMEM((peers, HEAD, rows), BF16),
            pltpu.VMEM((2 * HEAD, rows), BF16),
            pltpu.VMEM((peers + 1, 8, rows), F32),
            pltpu.VMEM((2, slots + FRESH, 2 * HEAD), BF16),
            pltpu.VMEM((2, HEAD + ONES, slots + FRESH), BF16),
            pltpu.VMEM((slots, HEAD), BF16),
            pltpu.VMEM(out_weight.shape, BF16),
            pltpu.VMEM((slots, rows), F32),
            pltpu.VMEM((slots, rows), F32),
            pltpu.VMEM((FRESH, rows), F32),
            pltpu.VMEM((FRESH, rows), F32),
            pltpu.VMEM((8, rows), F32),
            pltpu.VMEM((8, rows), F32),
            pltpu.VMEM((HEAD + ONES, rows), F32),
            pltpu.VMEM((8, rows), F32),
            pltpu.VMEM((HEAD + ONES, rows), F32),
            pltpu.VMEM((peers, HEAD, rows), BF16),
            pltpu.VMEM((peers, 8, rows), F32),
            pltpu.VMEM((peers, HEAD, rows), BF16),
            pltpu.VMEM((peers, 8, rows), F32),
            pltpu.VMEM((tokens, width), BF16),
            pltpu.VMEM((tp_size, tokens, span), BF16),
            pltpu.VMEM((tp_size, tokens, span), BF16),
            pltpu.VMEM((grid_tp[0], 2, tokens, span // 2), BF16),
            pltpu.VMEM((grid_tp[0], 2, tokens, span // 2), BF16),
            dma((3,)),
            dma((peers,)),
            dma((peers,)),
            dma((peers + 1,)),
            dma((peers + 1,)),
            dma((2,)),
            dma((2,)),
            dma((peers,)),
            dma((peers,)),
            dma((peers,)),
            dma((peers,)),
            dma((tp_size,)),
            dma((tp_size,)),
            dma((2 * grid_tp[0],)),
            dma((2 * grid_tp[0],)),
        ],
        compiler_params=pltpu.CompilerParams(
            collective_id=0, has_side_effects=True, vmem_limit_bytes=60 * 1024 * 1024
        ),
        cost_estimate=pl.CostEstimate(
            flops=4 * peers * rows * 2 * (slots + FRESH) * HEAD + 2 * tokens * width * out_weight.shape[1],
            bytes_accessed=2 * (out_weight.size + 2 * cache_keys.size),
            transcendentals=peers * rows * 2 * (slots + FRESH),
        ),
    )(
        queries,
        fresh_keys,
        fresh_values,
        positions.reshape(1, tokens),
        lengths,
        cache_keys,
        stored_values,
        out_weight,
    )


def solution(mesh):
    placed = (
        P("ctx", "tp"),
        P("ctx", "tp"),
        P("ctx", "tp"),
        P("ctx", "tp"),
        P("ctx", "tp"),
        P("ctx"),
        P("ctx"),
        P("tp", None),
    )
    sizes = (mesh.shape["ctx"], mesh.shape["tp"])
    return jax.shard_map(
        functools.partial(per_device, sizes=sizes),
        mesh=mesh,
        in_specs=placed,
        out_specs=P("ctx", "tp"),
        check_vma=False,
    )
```

```python
import functools
import math

import jax
import jax.numpy as jnp
from jax import lax
from jax.experimental import pallas as pl
from jax.experimental.pallas import tpu as pltpu
from jax.sharding import PartitionSpec as P

HEAD = 128
GROUP = 8
FRESH = 128
BLOCKS = 8
LOW = -1e30
FAR = 1e9
ONES = 16
F32 = jnp.float32
BF16 = jnp.bfloat16
UNIT = math.log2(math.e) / math.sqrt(HEAD)
MESH = pl.DeviceIdType.MESH


def kernel(
    grid_ctx,
    grid_tp,
    q_ref,
    fk_ref,
    fv_ref,
    pos_ref,
    len_ref,
    k_hbm,
    v_hbm,
    w_hbm,
    out_ref,
    qbuf,
    q_two,
    meta,
    kbuf,
    vbuf,
    v_raw,
    wbuf,
    s_a,
    s_b,
    f_a,
    f_b,
    peak,
    m_now,
    acc,
    m_own,
    acc_own,
    part_out,
    part_log,
    got_out,
    got_log,
    attended,
    proj_out,
    proj_got,
    relay_out,
    relay_got,
    local_sem,
    q_send,
    q_recv,
    meta_send,
    meta_recv,
    kv_send,
    kv_recv,
    out_send,
    out_recv,
    log_send,
    log_recv,
    proj_send,
    proj_recv,
    relay_send,
    relay_recv,
):
    nz, ny = grid_ctx
    tz, tx = grid_tp
    peers = nz * ny
    columns = tz * tx
    tokens = q_ref.shape[0]
    rows = tokens * GROUP
    slots = k_hbm.shape[0]
    block = slots // BLOCKS

    ctx = lax.axis_index("ctx")
    tp = lax.axis_index("tp")
    core = lax.rem(ctx, 2)
    chip = lax.div(ctx, 2)
    cz, cy = lax.div(chip, ny), lax.rem(chip, ny)
    pz, px = lax.div(tp, tx), lax.rem(tp, tx)
    partner = ctx + 1 - 2 * core

    def in_turn(k):
        return k + (1 - 2 * lax.rem(k, 2)) * lax.div(k + peers - 2, peers)

    def to_chip(turn):
        k = in_turn(turn)
        z = lax.rem(cz + nz - lax.div(k, ny), nz)
        y = lax.rem(cy + ny - lax.rem(k, ny), ny)
        return (z * ny + y) * 2 + core

    def from_chip(turn):
        k = in_turn(turn)
        z = lax.rem(cz + lax.div(k, ny), nz)
        y = lax.rem(cy + lax.rem(k, ny), ny)
        return (z * ny + y) * 2 + core

    def to_column(k):
        z = lax.rem(pz + lax.div(k, tx), tz)
        x = lax.rem(px + lax.rem(k, tx), tx)
        return z * tx + x

    def remote(src, dst, send, recv, where):
        return pltpu.make_async_remote_copy(
            src_ref=src, dst_ref=dst, send_sem=send, recv_sem=recv, device_id=where, device_id_type=MESH
        )

    def q_copy(k):
        return remote(qbuf.at[0], qbuf.at[k], q_send.at[k], q_recv.at[k], {"ctx": to_chip(k)})

    def meta_copy(k):
        return remote(meta.at[0], meta.at[k], meta_send.at[k], meta_recv.at[k], {"ctx": to_chip(k)})

    def meta_partner():
        return remote(meta.at[0], meta.at[peers], meta_send.at[peers], meta_recv.at[peers], {"ctx": partner})

    def k_partner():
        half = pl.ds(0, HEAD)
        return remote(kbuf.at[0, :, half], kbuf.at[1, :, half], kv_send.at[0], kv_recv.at[0], {"ctx": partner})

    def v_partner():
        return remote(vbuf.at[0], vbuf.at[1], kv_send.at[1], kv_recv.at[1], {"ctx": partner})

    def out_copy(k):
        return remote(part_out.at[k], got_out.at[k], out_send.at[k], out_recv.at[k], {"ctx": from_chip(k)})

    def log_copy(k):
        return remote(part_log.at[k], got_log.at[k], log_send.at[k], log_recv.at[k], {"ctx": from_chip(k)})

    def proj_copy(k):
        return remote(proj_out.at[k], proj_got.at[k], proj_send.at[k], proj_recv.at[k], {"tp": to_column(k)})

    def relay_copy(dz, side):
        to = to_column(1 if side == 0 else tx - 1)
        sems = relay_send.at[2 * dz + side], relay_recv.at[2 * dz + side]
        return remote(relay_out.at[dz, side], relay_got.at[dz, side], *sems, {"tp": to})

    k_load = pltpu.make_async_copy(k_hbm, kbuf.at[0, pl.ds(0, slots), pl.ds(0, HEAD)], local_sem.at[0])
    v_load = pltpu.make_async_copy(v_hbm, v_raw, local_sem.at[1])
    w_load = pltpu.make_async_copy(w_hbm, wbuf, local_sem.at[2])
    k_load.start()
    v_load.start()

    barrier = pltpu.get_barrier_semaphore()
    for k in range(1, peers):
        pl.semaphore_signal(barrier, inc=1, device_id={"ctx": to_chip(k)}, device_id_type=MESH)
    pl.semaphore_signal(barrier, inc=1, device_id={"ctx": partner}, device_id_type=MESH)
    for k in range(1, columns):
        pl.semaphore_signal(barrier, inc=1, device_id={"tp": to_column(k)}, device_id_type=MESH)

    stacked = jnp.concatenate([q_ref[:, h * HEAD : (h + 1) * HEAD].astype(F32) for h in range(GROUP)], axis=0)
    qbuf[0] = stacked.T.astype(BF16)
    meta[0] = jnp.broadcast_to(jnp.concatenate([pos_ref[...].astype(F32)] * GROUP, axis=1), (8, rows))
    spare = jnp.zeros((FRESH - tokens, HEAD), F32)
    fresh_keys = jnp.concatenate([fk_ref[...].astype(F32), spare], axis=0).astype(BF16)
    for half in range(2):
        kbuf[0, pl.ds(slots, FRESH), pl.ds(half * HEAD, HEAD)] = fresh_keys
    vbuf[0, pl.ds(0, HEAD), pl.ds(slots, FRESH)] = (
        jnp.concatenate([fv_ref[...].astype(F32), spare], axis=0).T.astype(BF16)
    )
    vbuf[0, pl.ds(HEAD, ONES), pl.ds(slots, FRESH)] = jnp.ones((ONES, FRESH), BF16)

    pl.semaphore_wait(barrier, peers - 1 + 1 + columns - 1)
    first_sends = min(3, peers)
    for k in range(1, first_sends):
        q_copy(k).start()
    for k in range(1, peers):
        meta_copy(k).start()
    meta_partner().start()

    filled = len_ref[0]
    k_load.wait()
    lead = kbuf[0, pl.ds(0, 16), pl.ds(0, HEAD)].astype(F32)[0:1]
    tidy = block // 2

    @pl.loop(0, slots // tidy)
    def _(c):
        at = pl.ds(pl.multiple_of(c * tidy, tidy), tidy)
        valid = lax.broadcasted_iota(jnp.int32, (tidy, HEAD), 0) + c * tidy < filled
        keys = jnp.where(valid, kbuf[0, at, pl.ds(0, HEAD)].astype(F32), lead).astype(BF16)
        kbuf[0, at, pl.ds(0, HEAD)] = keys
        kbuf[0, at, pl.ds(HEAD, HEAD)] = keys

    k_partner().start()
    v_load.wait()

    def tidy_values(b):
        at = pl.ds(b * block, block)
        valid = lax.broadcasted_iota(jnp.int32, (HEAD, block), 1) + b * block < filled
        vbuf[0, pl.ds(0, HEAD), at] = jnp.where(valid, v_raw[at, :].astype(F32).T, 0.0).astype(BF16)
        vbuf[0, pl.ds(HEAD, ONES), at] = jnp.where(valid[:ONES], 1.0, 0.0).astype(BF16)

    def split_queries(tile):
        scaled = qbuf[tile].astype(F32) * UNIT
        high = scaled.astype(BF16)
        q_two[pl.ds(0, HEAD), :] = high
        q_two[pl.ds(HEAD, HEAD), :] = (scaled - high.astype(F32)).astype(BF16)

    def fresh_scores(tile, shard, fresh):
        row = lax.broadcasted_iota(jnp.int32, (FRESH, FRESH), 0)
        lane = lax.broadcasted_iota(jnp.int32, (FRESH, FRESH), 1)
        spots = jnp.where(row == lane, meta[shard * peers, 0:1, pl.ds(0, FRESH)], 0.0)
        spot = jnp.where(row[:, :1] < tokens, jnp.sum(spots, axis=1, keepdims=True), FAR)
        s = jnp.dot(kbuf[shard, pl.ds(slots, FRESH), :], q_two[...], preferred_element_type=F32)
        s = jnp.where(spot <= meta[tile, 0:1, :], s, LOW)
        fresh[...] = s
        return s

    wide = min(1024, block)

    def top_of(s):
        return jnp.max(s.reshape(s.shape[0] // 8, 8, rows), axis=0)

    def phase(now, then, tile, shard_now, shard_then, beside=None):
        if now is not None:
            s_now, f_now = now
            m_old = m_now[0:1, :]
            m_new = jnp.maximum(m_old, jnp.max(peak[...], axis=0, keepdims=True))
            fade = jnp.exp2(m_old - m_new)
            m_now[...] = jnp.broadcast_to(m_new, (8, rows))
            p = jnp.exp2((f_now[...] - m_new).astype(BF16))
            add = jnp.dot(vbuf[shard_now, :, pl.ds(slots, FRESH)], p, preferred_element_type=F32)
            acc[...] = acc[...] * fade + add
        if then is not None:
            s_then, f_then = then
            top = top_of(fresh_scores(tile, shard_then, f_then))
        for b in range(BLOCKS):
            if beside is not None:
                beside(b)
            weights = []
            for c in range(block // wide):
                start = b * block + c * wide
                if then is not None:
                    s = jnp.dot(kbuf[shard_then, pl.ds(start, wide), :], q_two[...], preferred_element_type=F32)
                    s_then[pl.ds(start, wide), :] = s
                    top = jnp.maximum(top, top_of(s))
                if now is not None:
                    weights.append(jnp.exp2((s_now[pl.ds(start, wide), :] - m_new).astype(BF16)))
            if now is not None:
                acc[...] += jnp.dot(
                    vbuf[shard_now, :, pl.ds(b * block, block)],
                    jnp.concatenate(weights, axis=0),
                    preferred_element_type=F32,
                )
        if then is not None:
            peak[...] = top

    def clear():
        acc[...] = jnp.zeros_like(acc)
        m_now[...] = jnp.full_like(m_now, LOW)

    def finish(k):
        total = acc[pl.ds(HEAD, 8), :]
        part_out[k] = (acc[pl.ds(0, HEAD), :] / total[0:1]).astype(BF16)
        part_log[k] = m_now[...] + jnp.log(total) * math.log2(math.e)

    a, b = (s_a, f_a), (s_b, f_b)
    clear()
    split_queries(0)
    phase(None, a, 0, None, 0, tidy_values)
    v_partner().start()
    w_load.start()

    @pl.loop(0, peers)
    def _(t):
        shard = lax.rem(t, 2)
        tile = lax.rem(t + 1, peers)

        @pl.when(t + first_sends < peers)
        def _():
            q_copy(t + first_sends).start()

        @pl.when(t + 1 < peers)
        def _():
            q_copy(t + 1).wait_recv()
            meta_copy(t + 1).wait_recv()

        split_queries(tile)
        phase(a, b, tile, shard, shard)

        @pl.when(t == 0)
        def _():
            acc_own[...] = acc[...]
            m_own[...] = m_now[...]
            meta_partner().wait_recv()
            k_partner().wait_recv()

            @pl.loop(0, slots // tidy)
            def _(c):
                at = pl.ds(pl.multiple_of(c * tidy, tidy), tidy)
                kbuf[1, at, pl.ds(HEAD, HEAD)] = kbuf[1, at, pl.ds(0, HEAD)]

            kbuf[1, pl.ds(slots, FRESH), pl.ds(HEAD, HEAD)] = kbuf[1, pl.ds(slots, FRESH), pl.ds(0, HEAD)]

        @pl.when(t > 0)
        def _():
            finish(t)
            out_copy(t).start()
            log_copy(t).start()

        @pl.when(t + 1 < peers)
        def _():
            clear()
            phase(b, a, tile, shard, 1 - shard)

        @pl.when(t == 0)
        def _():
            v_partner().wait_recv()

        @pl.when(t + 1 == peers)
        def _():
            acc[...] = acc_own[...]
            m_now[...] = m_own[...]
            phase(b, None, None, shard, None)
            finish(0)

    for k in range(1, peers):
        out_copy(k).wait_recv()
        log_copy(k).wait_recv()
    logs = [part_log[0]] + [got_log[k] for k in range(1, peers)]
    top = functools.reduce(jnp.maximum, logs)
    shares = [jnp.exp2(log - top) for log in logs]
    whole = functools.reduce(jnp.add, shares)
    shares = [share / whole for share in shares]
    mixed = shares[0][0:1] * part_out[0].astype(F32)
    for k in range(1, peers):
        mixed += shares[k][0:1] * got_out[k].astype(F32)
    mixed = mixed.T.astype(BF16)
    for h in range(GROUP):
        attended[:, pl.ds(h * HEAD, HEAD)] = mixed[h * tokens : (h + 1) * tokens]

    w_load.wait()
    span = wbuf.shape[1] // columns

    def project(k):
        at = pl.ds(pl.multiple_of(to_column(k) * span, span), span)
        return jnp.dot(attended[...], wbuf[:, at], preferred_element_type=F32)

    def send_projected(k, terms):
        proj_out[k] = terms.astype(BF16)
        proj_copy(k).start()

    relayed = tx == 4
    side_span = span // 2
    if relayed:
        direct = [dz * tx for dz in range(tz - 1, 0, -1)]
        joined = [(dz, side) for dz in range(tz - 1, -1, -1) for side in range(2)]
        for dz in range(tz - 1, -1, -1):
            terms = project(dz * tx + 2).astype(BF16)
            for side in range(2):
                relay_out[dz, side] = terms[:, side * side_span : (side + 1) * side_span]
                relay_copy(dz, side).start()
    else:
        direct = list(range(columns - 1, 0, -1))
        joined = []
    for k in direct:
        send_projected(k, project(k))
    for dz, side in joined:
        k = dz * tx + (1 if side == 0 else tx - 1)
        terms = project(k)
        relay_copy(dz, side).wait_recv()
        left, right = terms[:, :side_span], terms[:, side_span:]
        more = relay_got[dz, side].astype(F32)
        halves = [left + more, right] if side == 0 else [left, right + more]
        send_projected(k, jnp.concatenate(halves, axis=1))
    sent = direct + [dz * tx + (1 if side == 0 else tx - 1) for dz, side in joined]

    result = project(0)
    for k in sent:
        proj_copy(k).wait_recv()
        result += proj_got[k].astype(F32)
    out_ref[...] = result.astype(BF16)

    for k in range(1, peers):
        q_copy(k).wait_send()
        meta_copy(k).wait_send()
        out_copy(k).wait_send()
        log_copy(k).wait_send()
    meta_partner().wait_send()
    k_partner().wait_send()
    v_partner().wait_send()
    for k in sent:
        proj_copy(k).wait_send()
    for dz, side in joined:
        relay_copy(dz, side).wait_send()


def grid_of(count):
    return (2, count // 2) if count > 4 else (1, count)


def per_device(queries, cache_keys, stored_values, fresh_keys, fresh_values, positions, lengths, out_weight, sizes):
    ctx_size, tp_size = sizes
    grid_ctx, grid_tp = grid_of(ctx_size // 2), grid_of(tp_size)
    peers = ctx_size // 2
    tokens, width = queries.shape
    rows = tokens * GROUP
    slots = cache_keys.shape[0]
    span = out_weight.shape[1] // tp_size
    vmem = pl.BlockSpec(memory_space=pltpu.VMEM)
    anywhere = pl.BlockSpec(memory_space=pl.ANY)
    dma = pltpu.SemaphoreType.DMA
    return pl.pallas_call(
        functools.partial(kernel, grid_ctx, grid_tp),
        out_shape=jax.ShapeDtypeStruct((tokens, span), BF16),
        in_specs=[vmem, vmem, vmem, vmem, pl.BlockSpec(memory_space=pltpu.SMEM), anywhere, anywhere, anywhere],
        out_specs=vmem,
        scratch_shapes=[
            pltpu.VMEM((peers, HEAD, rows), BF16),
            pltpu.VMEM((2 * HEAD, rows), BF16),
            pltpu.VMEM((peers + 1, 8, rows), F32),
            pltpu.VMEM((2, slots + FRESH, 2 * HEAD), BF16),
            pltpu.VMEM((2, HEAD + ONES, slots + FRESH), BF16),
            pltpu.VMEM((slots, HEAD), BF16),
            pltpu.VMEM(out_weight.shape, BF16),
            pltpu.VMEM((slots, rows), F32),
            pltpu.VMEM((slots, rows), F32),
            pltpu.VMEM((FRESH, rows), F32),
            pltpu.VMEM((FRESH, rows), F32),
            pltpu.VMEM((8, rows), F32),
            pltpu.VMEM((8, rows), F32),
            pltpu.VMEM((HEAD + ONES, rows), F32),
            pltpu.VMEM((8, rows), F32),
            pltpu.VMEM((HEAD + ONES, rows), F32),
            pltpu.VMEM((peers, HEAD, rows), BF16),
            pltpu.VMEM((peers, 8, rows), F32),
            pltpu.VMEM((peers, HEAD, rows), BF16),
            pltpu.VMEM((peers, 8, rows), F32),
            pltpu.VMEM((tokens, width), BF16),
            pltpu.VMEM((tp_size, tokens, span), BF16),
            pltpu.VMEM((tp_size, tokens, span), BF16),
            pltpu.VMEM((grid_tp[0], 2, tokens, span // 2), BF16),
            pltpu.VMEM((grid_tp[0], 2, tokens, span // 2), BF16),
            dma((3,)),
            dma((peers,)),
            dma((peers,)),
            dma((peers + 1,)),
            dma((peers + 1,)),
            dma((2,)),
            dma((2,)),
            dma((peers,)),
            dma((peers,)),
            dma((peers,)),
            dma((peers,)),
            dma((tp_size,)),
            dma((tp_size,)),
            dma((2 * grid_tp[0],)),
            dma((2 * grid_tp[0],)),
        ],
        compiler_params=pltpu.CompilerParams(
            collective_id=0, has_side_effects=True, vmem_limit_bytes=60 * 1024 * 1024
        ),
        cost_estimate=pl.CostEstimate(
            flops=4 * peers * rows * 2 * (slots + FRESH) * HEAD + 2 * tokens * width * out_weight.shape[1],
            bytes_accessed=2 * (out_weight.size + 2 * cache_keys.size),
            transcendentals=peers * rows * 2 * (slots + FRESH),
        ),
    )(
        queries,
        fresh_keys,
        fresh_values,
        positions.reshape(1, tokens),
        lengths,
        cache_keys,
        stored_values,
        out_weight,
    )


def solution(mesh):
    placed = (
        P("ctx", "tp"),
        P("ctx", "tp"),
        P("ctx", "tp"),
        P("ctx", "tp"),
        P("ctx", "tp"),
        P("ctx"),
        P("ctx"),
        P("tp", None),
    )
    sizes = (mesh.shape["ctx"], mesh.shape["tp"])
    return jax.shard_map(
        functools.partial(per_device, sizes=sizes),
        mesh=mesh,
        in_specs=placed,
        out_specs=P("ctx", "tp"),
        check_vma=False,
    )
```
